32 devices in a mesh: grp: 2 (over x), pi: 16 (over z, y, core).
Axes of the slice: x: 2, y: 2, z: 4, core: 2. Of those that a mesh axis runs over, the one named last changes fastest.
Arguments:
- left: bfloat16 [128, 1024], P(('grp', 'pi')), parts along dimension 0, may hold values from -6 to 6
- right: bfloat16 [128, 1024], P(('grp', 'pi')), parts along dimension 0, may hold values from -6 to 6
- depth: int32 [128], P(('grp', 'pi')), parts along dimension 0, may hold values from 1 to 32
- w_out: bfloat16 [1024, 128], replicated, may hold values from -0.1875 to 0.1875
- bias: float32 [128], replicated, may hold values from -4 to 4
- pair_cot: bfloat16 [128, 64, 128], P(('grp', 'pi')), parts along dimension 0, may hold values from -6 to 6
Outputs:
- pair_update: bfloat16 [128, 64, 128], P(('grp', 'pi')), parts along dimension 0
- grad_left: float32 [128, 1024], P(('grp', 'pi')), parts along dimension 0
- grad_right: float32 [128, 1024], P(('grp', 'pi')), parts along dimension 0
- grad_w: float32 [2048, 128], P('grp'), parts along dimension 0
- grad_bias: float32 [256], P('grp'), parts along dimension 0
The draws below stay inside these ranges and needn't reach their ends.
There are 2 independent parts, one for each index of `grp`. The reference program is written for one: setup_inputs(seed, part) draws one part's arguments, and reference() takes and returns one part's arrays. A program takes and returns all parts, laid end to end along the dimension named above; an argument that names none is the same for every part. Nothing has to cross between parts.
All inputs are finite; a program needn't handle non-finite values.
Results may differ from the reference program's by a relative error of at most 0.0034.
Values may be sent and summed in bfloat16 or wider, within the bound.
No kernel may reach another device: no remote copies, remote signals or barrier semaphores. Data moves between devices by JAX's collectives and lax.ppermute only.
A program may use at most 64 MiB of HBM per device.

```python
import math
import jax
import jax.numpy as jnp
from jax import lax

C = 32
CZ = 128
ROWS = 32
N = 64


def with_ends(drawn, key, least, largest):
    longest = drawn.shape.index(max(drawn.shape))
    spots = []
    for shift in (0, 1):
        where = [jax.random.randint(jax.random.fold_in(key, axis), (), 0, length) for axis, length in enumerate(drawn.shape)]
        where[longest] = (where[longest] + shift) % drawn.shape[longest]
        spots.append(tuple(where))
    return drawn.at[spots[0]].set(least).at[spots[1]].set(largest)


def raised(drawn, stream_key, source, target, shards_of, factor):
    def block_of(axis_at):
        return (jnp.arange(drawn.shape[axis_at]) // (drawn.shape[axis_at] // shards_of)).reshape((-1,) + (1,) * (drawn.ndim - 1 - axis_at))

    first = jax.random.permutation(stream_key, shards_of)[block_of(target)]
    second = (block_of(target) + shards_of // 2) % shards_of
    return jnp.where((block_of(source) == first) | (block_of(source) == second), factor * drawn, drawn)


def levels(stream_key, extent, pieces, smallest, high):
    gain = 1.0
    for dim, blocks in pieces:
        draws = jax.random.uniform(jax.random.fold_in(jax.random.fold_in(stream_key, 6), dim), (blocks,), jnp.float32, smallest / len(pieces), high / len(pieces))
        gain = gain * jnp.repeat(jnp.exp(draws), extent[dim] // blocks).reshape((-1,) + (1,) * (len(extent) - 1 - dim))
    return gain


def bell_draw(own_key, extent, width, most, split=(), held_as=jnp.bfloat16):
    drawn = jax.random.normal(own_key, extent, jnp.float32) * width
    if len(split) > 0:
        drawn = levels(own_key, extent, split, -0.22, 0.18) * drawn
    return jnp.clip(drawn, min=-most, max=most).astype(held_as)


def noise_with(rng, extent, scale, reach, shards, heavy, kind=jnp.bfloat16):
    entries = scale * jax.random.normal(rng, extent, jnp.float32)
    if shards:
        entries = entries * levels(rng, extent, shards, -0.22, 0.18)
    return jnp.clip(raised(entries, jax.random.fold_in(rng, 3), *heavy), -reach, reach).astype(kind)


def setup_inputs(seed: int = 0, part: int = 0) -> dict:
    arg_keys = jax.random.split(jax.random.key(seed), 7)
    part_splits = jax.random.split(jax.random.fold_in(arg_keys[6], part), 7)
    return {
        "left": bell_draw(part_splits[0], (N, ROWS * C), 1.0, 6.0, ((0, 16),)),
        "right": bell_draw(part_splits[1], (N, ROWS * C), 1.0, 6.0, ((0, 16),)),
        "depth": with_ends(jax.random.randint(part_splits[2], (N,), 1, ROWS + 1), jax.random.fold_in(part_splits[2], 1), 1, ROWS).astype(jnp.int32),
        "w_out": bell_draw(arg_keys[3], (C * C, CZ), (C * C) ** -0.5, 0.1875),
        "bias": bell_draw(arg_keys[4], (CZ,), 1.0, 4.0, (), jnp.float32),
        "pair_cot": noise_with(part_splits[5], (N, N, CZ), 1.0, 6.0, ((0, 16),), (0, 1, 16, 2.0)),
    }


epsilon = 1e-3


def reference(left, right, depth, w_out, bias, pair_cot):
    row_ids = jnp.arange(ROWS, dtype=jnp.int32)
    mask = (row_ids[None, :] < depth[:, None]).astype(jnp.bfloat16)
    left_masked = left.reshape(N, ROWS, C) * mask[:, :, None]
    right_masked = right.reshape(N, ROWS, C) * mask[:, :, None]
    block = math.gcd(N, 32)
    blocks = N // block

    def one_block(carry, block_index):
        weight_acc, bias_acc, right_acc = carry
        begin = (block_index * block).astype(jnp.int32)
        left_block = lax.dynamic_slice_in_dim(left_masked, begin, block, 0)
        depth_block = lax.dynamic_slice_in_dim(depth, begin, block, 0)
        mask_block = lax.dynamic_slice_in_dim(mask, begin, block, 0)
        cot_block = lax.dynamic_slice_in_dim(pair_cot, begin, block, 0)
        count = epsilon + jnp.minimum(depth_block[:, None], depth[None, :]).astype(jnp.float32)
        outer = jnp.einsum("isc,jsd->ijcd", left_block.astype(jnp.float32), right_masked.astype(jnp.float32))
        outer = (outer / count[:, :, None, None]).reshape(block, N, C * C).astype(jnp.bfloat16)
        update = (jnp.dot(outer, w_out, preferred_element_type=jnp.float32) + bias).astype(jnp.bfloat16)
        weight_acc = weight_acc + jnp.dot(outer.reshape(-1, C * C).T, cot_block.reshape(-1, CZ), preferred_element_type=jnp.float32)
        bias_acc = bias_acc + jnp.sum(cot_block, axis=(0, 1), dtype=jnp.float32)
        grad_pair = jnp.dot(cot_block, w_out.T, preferred_element_type=jnp.float32) / count[:, :, None]
        grad_pair = grad_pair.astype(jnp.bfloat16).reshape(block, N, C, C).astype(jnp.float32)
        left_grad = jnp.einsum("ijcd,jsd->isc", grad_pair, right_masked.astype(jnp.float32)) * mask_block[:, :, None]
        right_acc = right_acc + jnp.einsum("ijcd,isc->jsd", grad_pair, left_block.astype(jnp.float32))
        return (weight_acc, bias_acc, right_acc), (update, left_grad)

    init = (jnp.zeros((C * C, CZ), jnp.float32), jnp.zeros((CZ,), jnp.float32), jnp.zeros((N, ROWS, C), jnp.float32))
    carry, stacked = lax.scan(one_block, init, jnp.arange(blocks, dtype=jnp.int32))
    weight_acc, bias_acc, right_acc = carry
    updates, left_grads = stacked
    pair_update = updates.reshape(N, N, CZ)
    grad_left = left_grads.reshape(N, ROWS * C)
    grad_right = (right_acc * mask[:, :, None]).reshape(N, ROWS * C)
    return pair_update, grad_left, grad_right, weight_acc, bias_acc
```

```python
import functools
import math

import jax
import jax.numpy as jnp
from jax import lax
from jax.experimental import pallas as pl
from jax.experimental.pallas import tpu as pltpu
from jax.sharding import PartitionSpec as P

C = 32
LANES = 128
CORES = 2


epsilon = 0.001

F32 = jnp.float32
BF16 = jnp.bfloat16


def iota(shape, dim):
    return lax.broadcasted_iota(jnp.int32, shape, dim)


def dot(x, y, contract_x, contract_y):
    return lax.dot_general(
        x, y, (((contract_x,), (contract_y,)), ((), ())), preferred_element_type=F32
    )


def sum_kernel(rows, own_ref, other_ref, w_ref, right_ref, bias_ref):
    wide = w_ref.shape[0]
    w_ref[...] = own_ref[:wide, :] + other_ref[:wide, :]
    core = lax.rem(lax.axis_index("pi"), CORES)
    tiles = right_ref.shape[1] // LANES
    begin = pl.multiple_of(wide + core * rows * tiles, 8)
    part = own_ref[pl.ds(begin, rows * tiles), :] + other_ref[pl.ds(begin, rows * tiles), :]
    for row in range(rows):
        for tile in range(tiles):
            at = row * tiles + tile
            right_ref[row : row + 1, tile * LANES : (tile + 1) * LANES] = part[at : at + 1, :]
    last = wide + CORES * rows * tiles
    bias_ref[...] = own_ref[last : last + 1, :] + other_ref[last : last + 1, :]


def main_kernel(sizes, *refs):
    rows, total, pieces, depth_rows = sizes
    piece = refs[:pieces]
    w_ref, w_swap_ref, bias_ref = refs[pieces : pieces + 3]
    update_ref, left_ref, partial_ref = refs[pieces + 3 : pieces + 6]
    (
        right_all, turned, spread, left_all, left_wide, cots, inverse, outer, outer_own,
        window, picked, weights, g_left, g_right, stage,
    ) = refs[pieces + 6 :]
    chip_rows = CORES * rows
    pairs = rows * total
    tiles = C * C // LANES
    per_tile = LANES // total
    group = LANES // C
    me = lax.axis_index("pi")
    chip = me // CORES
    at_left = pairs
    at_right = pairs + C
    at_depth = at_right + (tiles + 1) * chip_rows

    for m in range(pieces):
        block = piece[m][at_right : at_right + depth_rows, :].astype(F32)
        for tile in range(tiles + 1):
            right_all[tile, m * chip_rows : (m + 1) * chip_rows, :] = block[
                tile * chip_rows : (tile + 1) * chip_rows
            ]
        left_all[m * C : (m + 1) * C, :] = piece[m][at_left : at_left + C, :]
        left_wide[m * C : (m + 1) * C, :] = piece[m][at_left : at_left + C, :].astype(F32)
        cots[m * pairs : (m + 1) * pairs, :] = piece[m][:pairs, :]
    place = lax.bitwise_xor(iota((total, LANES), 0), me * rows) == lax.rem(
        iota((total, LANES), 1), total
    )
    place = place.astype(F32).astype(BF16)
    for tile in range(tiles):
        turned[tile * LANES : (tile + 1) * LANES, :] = dot(
            right_all[tile].astype(BF16), place, 0, 0
        )
    depth_all = right_all[tiles].astype(BF16)
    depth_lane = dot(depth_all, place, 0, 0)

    for m in range(pieces):
        block = piece[m][at_right : at_right + depth_rows, :].astype(F32)
        for tile in range(pairs // LANES):
            at = at_depth - at_right + tile
            least = jnp.minimum(block[at : at + 1, :], depth_lane[:1, :])
            inverse[m * C : (m + 1) * C, tile * LANES : (tile + 1) * LANES] = jnp.broadcast_to(
                1.0 / (epsilon + least), (C, LANES)
            )

    alignment = spread.shape[0] // rows
    alive = iota((alignment, LANES), 0).astype(F32) < depth_lane[:alignment, :]
    part_of = iota((alignment, LANES), 1) // total
    keep = [jnp.where(alive & (part_of == k), 1.0, 0.0).astype(F32) for k in range(per_tile)]
    nothing = jnp.zeros((alignment, LANES), BF16)
    for d in range(C):
        block = turned[pl.ds(d, alignment, stride=C), :]
        kept = [(block * keep[k]).astype(BF16) for k in range(per_tile)]
        for i in range(rows):
            for tile in range(pairs // LANES):
                spread[
                    i * alignment : (i + 1) * alignment,
                    d * pairs + tile * LANES : d * pairs + (tile + 1) * LANES,
                ] = kept[i % per_tile] if i // per_tile == tile else nothing

    chunk = outer.shape[0] // C

    def some_channels(step, carry):
        for k in range(chunk):
            d = step * chunk + k
            begin = pl.multiple_of(d * pairs, pairs)
            o = dot(left_all[...], spread[:, pl.ds(begin, pairs)], 1, 0)
            o = (o * inverse[...]).astype(BF16)
            for m in range(pieces):
                outer[k * C : (k + 1) * C, m * pairs : (m + 1) * pairs] = o[m * C : (m + 1) * C, :]
        own_at = pl.multiple_of(step * chunk * C, chunk * C)
        outer_own[pl.ds(own_at, chunk * C), :] = outer[:, :pairs]
        grad = dot(outer[...], cots[...], 1, 0)
        for k in range(chunk):
            partial_ref[pl.ds(step * chunk + k, C, stride=C), :] = grad[k * C : (k + 1) * C, :]
        return carry

    lax.fori_loop(0, C // chunk, some_channels, 0)
    wide = C * C
    last = wide + chip_rows * tiles
    partial_ref[last : last + 8, :] = dot(
        jnp.ones((8, pieces * pairs), BF16), cots[...], 1, 0
    )

    half = lax.rem(chip, 16 // chip_rows)
    for m in range(pieces):
        for i in range(rows):
            begin = i * total + chip * chip_rows - half * chip_rows
            two = piece[m][pl.ds(pl.multiple_of(begin, 16), 16), :].astype(F32)
            one = two[:chip_rows]
            for k in range(1, 16 // chip_rows):
                one = jnp.where(half == k, two[k * chip_rows : (k + 1) * chip_rows], one)
            at = (i * pieces + m) * chip_rows
            window[at : at + chip_rows, :] = one
    mine = rows * pieces
    for j in range(chip_rows):
        picked[j * mine : (j + 1) * mine, :] = window[
            pl.ds(j, mine, stride=chip_rows), :
        ].astype(BF16)
    count_lanes = chip_rows * mine
    row = iota((total, count_lanes), 0)
    lane = iota((total, count_lanes), 1)
    own_lane = lax.rem(lane, mine)
    from_i = row == lax.rem(own_lane, pieces) * chip_rows + own_lane // pieces
    from_j = lax.bitwise_xor(row, me * rows) == chip * chip_rows + lane // mine
    depth_i = dot(depth_all, from_i.astype(F32).astype(BF16), 0, 0)[:8, :]
    depth_j = dot(depth_all, from_j.astype(F32).astype(BF16), 0, 0)[:8, :]
    inverse_right = (1.0 / (epsilon + jnp.minimum(depth_i, depth_j)))[:1, :]
    for c in range(C):
        g = dot(w_ref[c * C : (c + 1) * C, :], picked[...], 1, 1)
        g = (g * inverse_right).astype(BF16)
        for k in range(count_lanes // LANES):
            g_right[k * C : (k + 1) * C, c * LANES : (c + 1) * LANES] = g[
                :, k * LANES : (k + 1) * LANES
            ]
        feature = left_wide[pl.ds(c, pieces, stride=C), :]
        turns = [feature] + [pltpu.roll(feature, k * alignment, 1) for k in range(1, rows)]
        block_of = iota((pieces, LANES), 1) // alignment
        for j in range(group):
            both = jnp.concatenate(
                [jnp.where(block_of == j, turns[(j - i) % rows], 0.0) for i in range(rows)], 0
            )
            at = c * LANES + j * mine
            weights[at : at + mine, :] = both.astype(BF16)
    right_grad = dot(g_right[...], weights[...], 1, 0)
    in_tile = iota((8, LANES), 1) // C
    row_of = (iota((8, LANES), 0) * group + in_tile).astype(F32)
    for k in range(count_lanes // LANES):
        part = right_grad[k * C : (k + 1) * C, :]
        stage[...] = jnp.concatenate([part] * group, 0).T
        for j in range(group):
            flat = jnp.zeros((8, LANES), F32)
            for q in range(group):
                flat = jnp.where(
                    in_tile == q, stage[pl.ds(j * alignment + q, tiles, stride=group), :], flat
                )
            residue = lax.bitwise_xor(k * group + j, lax.rem(me, CORES) * rows)
            depth = right_all[tiles, pl.ds(residue, 1), :]
            at = wide + (k * group + j) * tiles
            partial_ref[at : at + tiles, :] = jnp.where(row_of < depth, flat, 0.0)

    update = dot(outer_own[...], w_swap_ref[...], 0, 0)
    update_ref[...] = (update + bias_ref[...]).astype(BF16)
    for d in range(C):
        g = dot(w_swap_ref[d * C : (d + 1) * C, :], piece[0][:pairs, :], 1, 1)
        g_left[:, d * pairs : (d + 1) * pairs] = (g * inverse[:C, :]).astype(BF16)
    left_grad = dot(g_left[...], spread[...], 1, 1)
    stage[...] = jnp.concatenate([left_grad] * group, 0).T
    for i in range(rows):
        flat = jnp.zeros((8, LANES), F32)
        for q in range(group):
            flat = jnp.where(
                in_tile == q, stage[pl.ds(i * alignment + q, tiles, stride=group), :], flat
            )
        flat = jnp.where(row_of < right_all[tiles, i : i + 1, :], flat, 0.0)
        for tile in range(tiles):
            left_ref[i : i + 1, tile * LANES : (tile + 1) * LANES] = flat[tile : tile + 1, :]


def swap(x, mask, size):
    return lax.ppermute(x, "pi", [(i, i ^ mask) for i in range(size)])


def gathered(left, right, depth, w_out, bias, pair_cot):
    rows, width = left.shape
    alignment = width // C
    total, channels = pair_cot.shape[1:]
    size = lax.axis_size("pi")
    pieces = size // CORES
    pairs = rows * total
    chip_rows = CORES * rows
    tiles = width // LANES
    depth_wide = jnp.broadcast_to(depth.astype(BF16)[:, None], (rows, LANES))
    right_own = jnp.concatenate([right, depth_wide], 1)
    right_chip = jnp.concatenate([right_own, swap(right_own, 1, size)], 0)
    right_chip = right_chip.reshape(chip_rows, tiles + 1, LANES).swapaxes(0, 1)
    row_ids = jnp.arange(alignment, dtype=jnp.int32)
    own_mask = (row_ids[None, :] < depth[:, None]).astype(BF16)
    own_left = left.reshape(rows, alignment, C) * own_mask[:, :, None]
    depth_pairs = jnp.broadcast_to(depth.astype(BF16)[:, None], (rows, total))
    used = pairs + C + (tiles + 1) * chip_rows + pairs // LANES
    spare = -used % 16
    payload = jnp.concatenate(
        [
            pair_cot.reshape(pairs, channels),
            own_left.transpose(2, 0, 1).reshape(C, LANES),
            right_chip.reshape(-1, LANES),
            depth_pairs.reshape(-1, LANES),
            jnp.zeros((spare, LANES), BF16),
        ],
        0,
    )
    far = [payload] + [swap(payload, mask, size) for mask in range(2 * CORES, size, 2 * CORES)]
    near = [swap(x, CORES, size) for x in far]
    arrived = [x for both in zip(far, near) for x in both]
    w_swap = w_out.reshape(C, C, channels).swapaxes(0, 1).reshape(C * C, channels)
    depth_rows = used + spare - pairs - C
    partial_rows = C * C + chip_rows * tiles + 8
    count_lanes = chip_rows * rows * pieces
    chunk = 8
    update, grad_left, partial = pl.pallas_call(
        functools.partial(main_kernel, (rows, total, pieces, depth_rows)),
        out_shape=(
            jax.ShapeDtypeStruct((pairs, channels), BF16),
            jax.ShapeDtypeStruct((rows, width), F32),
            jax.ShapeDtypeStruct((partial_rows, LANES), F32),
        ),
        scratch_shapes=[
            pltpu.VMEM((tiles + 1, total, LANES), F32),
            pltpu.VMEM((width, LANES), F32),
            pltpu.VMEM((rows * alignment, C * pairs), BF16),
            pltpu.VMEM((pieces * C, LANES), BF16),
            pltpu.VMEM((pieces * C, LANES), F32),
            pltpu.VMEM((pieces * pairs, channels), BF16),
            pltpu.VMEM((pieces * C, pairs), F32),
            pltpu.VMEM((chunk * C, pieces * pairs), BF16),
            pltpu.VMEM((C * C, pairs), BF16),
            pltpu.VMEM((count_lanes, channels), F32),
            pltpu.VMEM((count_lanes, channels), BF16),
            pltpu.VMEM((C * LANES, LANES), BF16),
            pltpu.VMEM((C, C * pairs), BF16),
            pltpu.VMEM((count_lanes // LANES * C, C * LANES), BF16),
            pltpu.VMEM((LANES, LANES), F32),
        ],
        compiler_params=pltpu.CompilerParams(vmem_limit_bytes=40 * 1024 * 1024),
    )(*arrived, w_out, w_swap, bias.reshape(1, channels))
    other = swap(partial, 1, size)
    grad_w, grad_right, grad_bias = pl.pallas_call(
        functools.partial(sum_kernel, rows),
        out_shape=(
            jax.ShapeDtypeStruct((C * C, channels), F32),
            jax.ShapeDtypeStruct((rows, width), F32),
            jax.ShapeDtypeStruct((1, channels), F32),
        ),
    )(partial, other)
    return (
        update.reshape(rows, total, channels),
        grad_left,
        grad_right,
        grad_w,
        grad_bias.reshape(channels),
    )


def gathers(left, pair_cot, w_out):
    rows, width = left.shape
    total, channels = pair_cot.shape[1:]
    size = lax.axis_size("pi")
    gather_bytes = size * pair_cot.size * 2
    reduce_bytes = 2 * w_out.size * 4
    return (
        gather_bytes <= reduce_bytes
        and size >= 2 * CORES
        and size & (size - 1) == 0
        and rows & (rows - 1) == 0
        and channels == LANES
        and rows * (width // C) == LANES
        and LANES % total == 0
        and width == C * C == 8 * LANES
        and rows * CORES == 8
        and (rows * size // CORES) * (LANES // C) == LANES
    )


def local(left, right, depth, w_out, bias, pair_cot):
    if gathers(left, pair_cot, w_out):
        return gathered(left, right, depth, w_out, bias, pair_cot)
    return reduced(left, right, depth, w_out, bias, pair_cot)


def reduced(left, right, depth, w_out, bias, pair_cot):
    rows = left.shape[0]
    width = left.shape[1]
    alignment = width // C
    total = pair_cot.shape[1]
    channels = w_out.shape[1]
    row_ids = jnp.arange(alignment, dtype=jnp.int32)
    own_mask = (row_ids[None, :] < depth[:, None]).astype(jnp.bfloat16)
    own_left = left.reshape(rows, alignment, C) * own_mask[:, :, None]
    w_back = w_out.T
    pair_cols = lax.all_to_all(pair_cot, "pi", split_axis=1, concat_axis=0, tiled=True)
    init = (
        jnp.zeros((rows, total, channels), jnp.bfloat16),
        jnp.zeros((rows, width), jnp.float32),
        jnp.zeros((C * C, channels), jnp.float32),
        jnp.zeros((channels,), jnp.float32),
    )
    carry = init
    start = jnp.int32(0)
    right_piece = lax.all_gather(right, "pi", axis=0, tiled=True)
    depth_piece = lax.all_gather(depth, "pi", axis=0, tiled=True)
    length = right_piece.shape[0]
    block = math.gcd(length, 256)
    for offset in range(0, length, block):
        begin = start + offset
        depth_block = depth_piece[offset : offset + block]
        mask_block = (row_ids[None, :] < depth_block[:, None]).astype(jnp.bfloat16)
        right_block = (
            right_piece[offset : offset + block].reshape(block, alignment, C)
            * mask_block[:, :, None]
        )
        count = epsilon + jnp.minimum(depth[:, None], depth_block[None, :]).astype(jnp.float32)
        outer = jnp.einsum(
            "isc,jsd->ijcd", own_left, right_block, preferred_element_type=jnp.float32
        )
        outer = (outer / count[:, :, None, None]).reshape(rows, block, C * C).astype(jnp.bfloat16)
        update = (jnp.dot(outer, w_out, preferred_element_type=jnp.float32) + bias).astype(
            jnp.bfloat16
        )
        cot_block = lax.dynamic_slice_in_dim(pair_cot, begin, block, 1)
        pair_out = lax.dynamic_update_slice(carry[0], update, (0, begin, 0))
        weight_acc = carry[2] + jnp.dot(
            outer.reshape(-1, C * C).T,
            cot_block.reshape(-1, channels),
            preferred_element_type=jnp.float32,
        )
        bias_acc = carry[3] + jnp.sum(cot_block, axis=(0, 1), dtype=jnp.float32)
        grad_pair = (
            jnp.dot(cot_block, w_back, preferred_element_type=jnp.float32) / count[:, :, None]
        )
        grad_pair = grad_pair.astype(jnp.bfloat16).reshape(rows, block, C, C)
        left_acc = carry[1] + jnp.einsum(
            "ijcd,jsd->isc", grad_pair, right_block, preferred_element_type=jnp.float32
        ).reshape(rows, width)
        carry = (pair_out, left_acc, weight_acc, bias_acc)
    pair_update = carry[0]
    left_acc = carry[1]
    accum = jnp.zeros((rows, width), jnp.float32)
    start = jnp.int32(0)
    left_piece = lax.all_gather(left, "pi", axis=0, tiled=True)
    depth_piece = lax.all_gather(depth, "pi", axis=0, tiled=True)
    length = left_piece.shape[0]
    block = math.gcd(length, 256)
    for offset in range(0, length, block):
        begin = start + offset
        depth_block = depth_piece[offset : offset + block]
        mask_block = (row_ids[None, :] < depth_block[:, None]).astype(jnp.bfloat16)
        left_block = (
            left_piece[offset : offset + block].reshape(block, alignment, C)
            * mask_block[:, :, None]
        )
        count = epsilon + jnp.minimum(depth_block[:, None], depth[None, :]).astype(jnp.float32)
        cot_block = lax.dynamic_slice_in_dim(pair_cols, begin, block, 0)
        grad_pair = (
            jnp.dot(cot_block, w_back, preferred_element_type=jnp.float32) / count[:, :, None]
        )
        grad_pair = grad_pair.astype(jnp.bfloat16).reshape(block, rows, C, C)
        accum = accum + jnp.einsum(
            "ijcd,isc->jsd", grad_pair, left_block, preferred_element_type=jnp.float32
        ).reshape(rows, width)
    grad_w, grad_bias = lax.psum((carry[2], carry[3]), "pi")
    grad_left = (left_acc.reshape(rows, alignment, C) * own_mask[:, :, None]).reshape(rows, width)
    grad_right = (accum.reshape(rows, alignment, C) * own_mask[:, :, None]).reshape(rows, width)
    return (pair_update, grad_left, grad_right, grad_w, grad_bias)


def solution(mesh):
    placed = (
        P(("grp", "pi"), None),
        P(("grp", "pi"), None),
        P(("grp", "pi")),
        P(),
        P(),
        P(("grp", "pi"), None, None),
    )
    return jax.shard_map(
        local,
        mesh=mesh,
        in_specs=placed,
        out_specs=(
            P(("grp", "pi"), None, None),
            P(("grp", "pi"), None),
            P(("grp", "pi"), None),
            P("grp", None),
            P("grp"),
        ),
        check_vma=False,
    )
```

```python
import functools
import math

import jax
import jax.numpy as jnp
from jax import lax
from jax.experimental import pallas as pl
from jax.experimental.pallas import tpu as pltpu
from jax.sharding import PartitionSpec as P

C = 32
LANES = 128
CORES = 2
SMALL = 8 * 2**20
LARGE = 24 * 2**20


epsilon = 0.001

F32 = jnp.float32
BF16 = jnp.bfloat16


def iota(shape, dim):
    return lax.broadcasted_iota(jnp.int32, shape, dim)


def dot(x, y, contract_x, contract_y):
    return lax.dot_general(
        x, y, (((contract_x,), (contract_y,)), ((), ())), preferred_element_type=F32
    )


def pack_kernel(
    left_ref, right_ref, cot_ref, depth_ref, bias_ref, w_ref,
    payload_ref, bias_out_ref, w_out_ref,
    left_here, right_here, depth_here, sems,
):
    rows, width = left_here.shape
    pairs = cot_ref.shape[0]
    total = pairs // rows
    alignment = width // C
    tiles = width // LANES
    group = LANES // C
    chip_rows = CORES * rows
    ends = (
        (depth_ref, depth_here),
        (left_ref, left_here),
        (right_ref, right_here),
        (cot_ref, payload_ref.at[:pairs, :]),
        (bias_ref, bias_out_ref),
        (w_ref, w_out_ref),
    )
    copies = [pltpu.make_async_copy(*pair, sems.at[k]) for k, pair in enumerate(ends)]
    for copy in copies:
        copy.start()
    for copy in copies[:3]:
        copy.wait()
    left = left_here[...].astype(F32)
    flat = jnp.concatenate([left[:, t * LANES : (t + 1) * LANES] for t in range(tiles)], 0)
    flat = flat.astype(BF16)
    row = iota((tiles * rows, LANES), 0)
    lane = iota((tiles * rows, LANES), 1)
    target = lax.rem(row, rows) * alignment + row // rows * group
    turned = jnp.zeros((C, LANES), F32)
    for q in range(group):
        place = (lane == target + q).astype(F32).astype(BF16)
        turned = turned + dot(flat, place, 0, 0)[q * C : (q + 1) * C, :]
    lane = iota((C, LANES), 1)
    depth = jnp.zeros((C, LANES), jnp.int32)
    for i in range(rows):
        depth = jnp.where(lane // alignment == i, depth_here[i], depth)
    turned = jnp.where(lax.rem(lane, alignment) < depth, turned, 0.0)
    payload_ref[pairs : pairs + C, :] = turned.astype(BF16)
    own = right_here[...].astype(F32)
    nothing = jnp.zeros((rows, LANES), F32)
    parts = []
    for t in range(tiles):
        parts += [own[:, t * LANES : (t + 1) * LANES], nothing]
    row = iota((chip_rows, LANES), 0)
    depth = jnp.zeros((chip_rows, LANES), jnp.int32)
    for i in range(rows):
        depth = jnp.where(row == i, depth_here[i], depth)
    parts.append(depth.astype(F32))
    lane = row * LANES + iota((chip_rows, LANES), 1)
    depth = jnp.zeros((chip_rows, LANES), jnp.int32)
    for i in range(rows):
        depth = jnp.where(lane // total == i, depth_here[i], depth)
    parts.append(depth.astype(F32))
    payload_ref[pairs + C :, :] = jnp.concatenate(parts, 0).astype(BF16)
    for copy in copies[3:]:
        copy.wait()


def add_kernel(pairs, payload_ref, right_ref, depth_ref, out_ref):
    rows, width = right_ref.shape
    tiles = width // LANES
    chip_rows = CORES * rows
    begin = pairs + C
    block = payload_ref[begin:, :].astype(F32)
    other = right_ref[...].astype(F32)
    row = iota((chip_rows, LANES), 0)
    parts = []
    for t in range(tiles):
        both = jnp.concatenate([other[:, t * LANES : (t + 1) * LANES]] * CORES, 0)
        parts.append(jnp.where(row < rows, block[t * chip_rows : (t + 1) * chip_rows], both))
    depth = jnp.broadcast_to(depth_ref[...].astype(F32), (chip_rows, rows))
    mine = iota((chip_rows, rows), 0) == iota((chip_rows, rows), 1) + rows
    depth = jnp.sum(jnp.where(mine, depth, 0.0), axis=1, keepdims=True)
    own = block[tiles * chip_rows : (tiles + 1) * chip_rows]
    parts.append(jnp.where(row < rows, own, jnp.broadcast_to(depth, (chip_rows, LANES))))
    parts.append(block[(tiles + 1) * chip_rows :])
    out_ref[begin:, :] = jnp.concatenate(parts, 0).astype(BF16)


def sum_kernel(rows, own_ref, other_ref, w_ref, right_ref, bias_ref):
    wide = w_ref.shape[0]
    w_ref[...] = own_ref[:wide, :] + other_ref[:wide, :]
    core = lax.rem(lax.axis_index("pi"), CORES)
    tiles = right_ref.shape[1] // LANES
    begin = pl.multiple_of(wide + core * rows * tiles, 8)
    part = own_ref[pl.ds(begin, rows * tiles), :] + other_ref[pl.ds(begin, rows * tiles), :]
    for row in range(rows):
        for tile in range(tiles):
            at = row * tiles + tile
            right_ref[row : row + 1, tile * LANES : (tile + 1) * LANES] = part[at : at + 1, :]
    last = wide + CORES * rows * tiles
    bias_ref[...] = own_ref[last : last + 1, :] + other_ref[last : last + 1, :]


def main_kernel(sizes, *refs):
    rows, total, pieces, depth_rows = sizes
    piece = refs[:pieces]
    w_ref, partial_ref, spread, outer_own, inverse_own, depth_own = refs[pieces : pieces + 6]
    (
        right_all, turned, left_all, left_wide, cots, inverse, outer, window, picked, weights,
        g_right, stage,
    ) = refs[pieces + 6 :]
    chip_rows = CORES * rows
    pairs = rows * total
    tiles = C * C // LANES
    per_tile = LANES // total
    group = LANES // C
    me = lax.axis_index("pi")
    chip = me // CORES
    at_left = pairs
    at_right = pairs + C
    at_depth = at_right + (tiles + 1) * chip_rows

    for m in range(pieces):
        block = piece[m][at_right : at_right + depth_rows, :].astype(F32)
        for tile in range(tiles + 1):
            right_all[tile, m * chip_rows : (m + 1) * chip_rows, :] = block[
                tile * chip_rows : (tile + 1) * chip_rows
            ]
        left_all[m * C : (m + 1) * C, :] = piece[m][at_left : at_left + C, :]
        left_wide[m * C : (m + 1) * C, :] = piece[m][at_left : at_left + C, :].astype(F32)
        cots[m * pairs : (m + 1) * pairs, :] = piece[m][:pairs, :]
    place = lax.bitwise_xor(iota((total, LANES), 0), me * rows) == lax.rem(
        iota((total, LANES), 1), total
    )
    place = place.astype(F32).astype(BF16)
    for tile in range(tiles):
        turned[tile * LANES : (tile + 1) * LANES, :] = dot(
            right_all[tile].astype(BF16), place, 0, 0
        )
    depth_all = right_all[tiles].astype(BF16)
    depth_lane = dot(depth_all, place, 0, 0)

    for m in range(pieces):
        block = piece[m][at_right : at_right + depth_rows, :].astype(F32)
        for tile in range(pairs // LANES):
            at = at_depth - at_right + tile
            least = jnp.minimum(block[at : at + 1, :], depth_lane[:1, :])
            inverse[m * C : (m + 1) * C, tile * LANES : (tile + 1) * LANES] = jnp.broadcast_to(
                1.0 / (epsilon + least), (C, LANES)
            )

    alignment = spread.shape[0] // rows
    alive = iota((alignment, LANES), 0).astype(F32) < depth_lane[:alignment, :]
    part_of = iota((alignment, LANES), 1) // total
    keep = [jnp.where(alive & (part_of == k), 1.0, 0.0).astype(F32) for k in range(per_tile)]
    nothing = jnp.zeros((alignment, LANES), BF16)
    for d in range(C):
        block = turned[pl.ds(d, alignment, stride=C), :]
        kept = [(block * keep[k]).astype(BF16) for k in range(per_tile)]
        for i in range(rows):
            for tile in range(pairs // LANES):
                spread[
                    i * alignment : (i + 1) * alignment,
                    d * pairs + tile * LANES : d * pairs + (tile + 1) * LANES,
                ] = kept[i % per_tile] if i // per_tile == tile else nothing

    chunk = outer.shape[0] // C

    def some_channels(step, carry):
        for k in range(chunk):
            d = step * chunk + k
            begin = pl.multiple_of(d * pairs, pairs)
            o = dot(left_all[...], spread[:, pl.ds(begin, pairs)], 1, 0)
            o = (o * inverse[...]).astype(BF16)
            for m in range(pieces):
                outer[k * C : (k + 1) * C, m * pairs : (m + 1) * pairs] = o[m * C : (m + 1) * C, :]
        own_at = pl.multiple_of(step * chunk * C, chunk * C)
        outer_own[pl.ds(own_at, chunk * C), :] = outer[:, :pairs]
        grad = dot(outer[...], cots[...], 1, 0)
        for k in range(chunk):
            partial_ref[pl.ds(step * chunk + k, C, stride=C), :] = grad[k * C : (k + 1) * C, :]
        return carry

    lax.fori_loop(0, C // chunk, some_channels, 0)
    wide = C * C
    last = wide + chip_rows * tiles
    partial_ref[last : last + 8, :] = dot(
        jnp.ones((8, pieces * pairs), BF16), cots[...], 1, 0
    )

    half = lax.rem(chip, 16 // chip_rows)
    for m in range(pieces):
        for i in range(rows):
            begin = i * total + chip * chip_rows - half * chip_rows
            two = piece[m][pl.ds(pl.multiple_of(begin, 16), 16), :].astype(F32)
            one = two[:chip_rows]
            for k in range(1, 16 // chip_rows):
                one = jnp.where(half == k, two[k * chip_rows : (k + 1) * chip_rows], one)
            at = (i * pieces + m) * chip_rows
            window[at : at + chip_rows, :] = one
    mine = rows * pieces
    for j in range(chip_rows):
        picked[j * mine : (j + 1) * mine, :] = window[
            pl.ds(j, mine, stride=chip_rows), :
        ].astype(BF16)
    count_lanes = chip_rows * mine
    row = iota((total, count_lanes), 0)
    lane = iota((total, count_lanes), 1)
    own_lane = lax.rem(lane, mine)
    from_i = row == lax.rem(own_lane, pieces) * chip_rows + own_lane // pieces
    from_j = lax.bitwise_xor(row, me * rows) == chip * chip_rows + lane // mine
    depth_i = dot(depth_all, from_i.astype(F32).astype(BF16), 0, 0)[:8, :]
    depth_j = dot(depth_all, from_j.astype(F32).astype(BF16), 0, 0)[:8, :]
    inverse_right = (1.0 / (epsilon + jnp.minimum(depth_i, depth_j)))[:1, :]
    for c in range(C):
        g = dot(w_ref[c * C : (c + 1) * C, :], picked[...], 1, 1)
        g = (g * inverse_right).astype(BF16)
        for k in range(count_lanes // LANES):
            g_right[k * C : (k + 1) * C, c * LANES : (c + 1) * LANES] = g[
                :, k * LANES : (k + 1) * LANES
            ]
        feature = left_wide[pl.ds(c, pieces, stride=C), :]
        turns = [feature] + [pltpu.roll(feature, k * alignment, 1) for k in range(1, rows)]
        block_of = iota((pieces, LANES), 1) // alignment
        for j in range(group):
            both = jnp.concatenate(
                [jnp.where(block_of == j, turns[(j - i) % rows], 0.0) for i in range(rows)], 0
            )
            at = c * LANES + j * mine
            weights[at : at + mine, :] = both.astype(BF16)
    right_grad = dot(g_right[...], weights[...], 1, 0)
    in_tile = iota((8, LANES), 1) // C
    row_of = (iota((8, LANES), 0) * group + in_tile).astype(F32)
    for k in range(count_lanes // LANES):
        part = right_grad[k * C : (k + 1) * C, :]
        stage[...] = jnp.concatenate([part] * group, 0).T
        for j in range(group):
            flat = jnp.zeros((8, LANES), F32)
            for q in range(group):
                flat = jnp.where(
                    in_tile == q, stage[pl.ds(j * alignment + q, tiles, stride=group), :], flat
                )
            residue = lax.bitwise_xor(k * group + j, lax.rem(me, CORES) * rows)
            depth = right_all[tiles, pl.ds(residue, 1), :]
            at = wide + (k * group + j) * tiles
            partial_ref[at : at + tiles, :] = jnp.where(row_of < depth, flat, 0.0)

    inverse_own[...] = inverse[:8, :]
    depth_own[...] = right_all[tiles, :8, :]


def own_kernel(
    rows, spread, outer_own, inverse_own, depth_own, payload_ref, w_swap_ref, bias_ref,
    update_ref, left_ref, g_left, stage,
):
    pairs = update_ref.shape[0]
    alignment = spread.shape[0] // rows
    tiles = left_ref.shape[1] // LANES
    group = LANES // C
    update = dot(outer_own[...], w_swap_ref[...], 0, 0)
    update_ref[...] = (update + bias_ref[...]).astype(BF16)
    for d in range(C):
        g = dot(w_swap_ref[d * C : (d + 1) * C, :], payload_ref[:pairs, :], 1, 1)
        g_left[:, d * pairs : (d + 1) * pairs] = (g * inverse_own[:1, :]).astype(BF16)
    left_grad = dot(g_left[...], spread[...], 1, 1)
    stage[...] = jnp.concatenate([left_grad] * group, 0).T
    in_tile = iota((8, LANES), 1) // C
    row_of = (iota((8, LANES), 0) * group + in_tile).astype(F32)
    for i in range(rows):
        flat = jnp.zeros((8, LANES), F32)
        for q in range(group):
            flat = jnp.where(
                in_tile == q, stage[pl.ds(i * alignment + q, tiles, stride=group), :], flat
            )
        flat = jnp.where(row_of < depth_own[i : i + 1, :], flat, 0.0)
        for tile in range(tiles):
            left_ref[i : i + 1, tile * LANES : (tile + 1) * LANES] = flat[tile : tile + 1, :]


def swap(x, mask, size):
    return lax.ppermute(x, "pi", [(i, i ^ mask) for i in range(size)])


def gathered(left, right, depth, w_out, bias, pair_cot):
    rows, width = left.shape
    alignment = width // C
    total, channels = pair_cot.shape[1:]
    size = lax.axis_size("pi")
    pieces = size // CORES
    pairs = rows * total
    chip_rows = CORES * rows
    tiles = width // LANES
    used = pairs + C + (tiles + 2) * chip_rows
    hbm = pl.BlockSpec(memory_space=pltpu.HBM)
    vmem = pl.BlockSpec(memory_space=pltpu.VMEM)
    right_other = swap(right, 1, size)
    depth_other = swap(depth, 1, size)
    given = (
        left, right, pair_cot.reshape(pairs, channels), depth, bias.reshape(1, channels), w_out,
    )
    payload, bias_row, w_here = pl.pallas_call(
        pack_kernel,
        out_shape=(
            pltpu.VMEM((used, LANES), BF16),
            pltpu.VMEM((1, channels), F32),
            pltpu.VMEM(w_out.shape, BF16),
        ),
        in_specs=[hbm] * 6,
        out_specs=(vmem, vmem, vmem),
        scratch_shapes=[
            pltpu.VMEM(left.shape, BF16),
            pltpu.VMEM(right.shape, BF16),
            pltpu.SMEM(depth.shape, jnp.int32),
            pltpu.SemaphoreType.DMA((6,)),
        ],
        compiler_params=pltpu.CompilerParams(vmem_limit_bytes=SMALL),
        cost_estimate=pl.CostEstimate(flops=10**9, bytes_accessed=2**20, transcendentals=0),
    )(*[pltpu.with_memory_space_constraint(x, pltpu.HBM) for x in given])
    payload = pl.pallas_call(
        functools.partial(add_kernel, pairs),
        out_shape=jax.ShapeDtypeStruct((used, LANES), BF16),
        input_output_aliases={0: 0},
        compiler_params=pltpu.CompilerParams(vmem_limit_bytes=SMALL),
    )(payload, right_other, depth_other.reshape(1, rows))
    far = [payload] + [swap(payload, mask, size) for mask in range(2 * CORES, size, 2 * CORES)]
    near = [swap(x, CORES, size) for x in far]
    arrived = [x for both in zip(far, near) for x in both]
    w_swap = w_here.reshape(C, C, channels).swapaxes(0, 1).reshape(C * C, channels)
    depth_rows = used - pairs - C
    partial_rows = C * C + chip_rows * tiles + 8
    count_lanes = chip_rows * rows * pieces
    chunk = 8
    partial, spread, outer_own, inverse_own, depth_own = pl.pallas_call(
        functools.partial(main_kernel, (rows, total, pieces, depth_rows)),
        out_shape=(
            jax.ShapeDtypeStruct((partial_rows, LANES), F32),
            jax.ShapeDtypeStruct((rows * alignment, C * pairs), BF16),
            jax.ShapeDtypeStruct((C * C, pairs), BF16),
            jax.ShapeDtypeStruct((8, pairs), F32),
            jax.ShapeDtypeStruct((8, LANES), F32),
        ),
        scratch_shapes=[
            pltpu.VMEM((tiles + 1, total, LANES), F32),
            pltpu.VMEM((width, LANES), F32),
            pltpu.VMEM((pieces * C, LANES), BF16),
            pltpu.VMEM((pieces * C, LANES), F32),
            pltpu.VMEM((pieces * pairs, channels), BF16),
            pltpu.VMEM((pieces * C, pairs), F32),
            pltpu.VMEM((chunk * C, pieces * pairs), BF16),
            pltpu.VMEM((count_lanes, channels), F32),
            pltpu.VMEM((count_lanes, channels), BF16),
            pltpu.VMEM((C * LANES, LANES), BF16),
            pltpu.VMEM((count_lanes // LANES * C, C * LANES), BF16),
            pltpu.VMEM((LANES, LANES), F32),
        ],
        compiler_params=pltpu.CompilerParams(vmem_limit_bytes=LARGE),
    )(*arrived, w_here)
    other = swap(partial, 1, size)
    update, grad_left = pl.pallas_call(
        functools.partial(own_kernel, rows),
        out_shape=(
            jax.ShapeDtypeStruct((pairs, channels), BF16),
            jax.ShapeDtypeStruct((rows, width), F32),
        ),
        scratch_shapes=[
            pltpu.VMEM((C, C * pairs), BF16),
            pltpu.VMEM((LANES, LANES), F32),
        ],
        compiler_params=pltpu.CompilerParams(vmem_limit_bytes=LARGE),
        cost_estimate=pl.CostEstimate(
            flops=8 * pairs * C * C * channels, bytes_accessed=4 * 2**20, transcendentals=0
        ),
    )(spread, outer_own, inverse_own, depth_own, payload, w_swap, bias_row)
    grad_w, grad_right, grad_bias = pl.pallas_call(
        functools.partial(sum_kernel, rows),
        out_shape=(
            jax.ShapeDtypeStruct((C * C, channels), F32),
            jax.ShapeDtypeStruct((rows, width), F32),
            jax.ShapeDtypeStruct((1, channels), F32),
        ),
        compiler_params=pltpu.CompilerParams(vmem_limit_bytes=SMALL),
    )(partial, other)
    return (
        update.reshape(rows, total, channels),
        grad_left,
        grad_right,
        grad_w,
        grad_bias.reshape(channels),
    )


def gathers(left, pair_cot, w_out):
    rows, width = left.shape
    total, channels = pair_cot.shape[1:]
    size = lax.axis_size("pi")
    gather_bytes = size * pair_cot.size * 2
    reduce_bytes = 2 * w_out.size * 4
    return (
        gather_bytes <= reduce_bytes
        and size >= 2 * CORES
        and size & (size - 1) == 0
        and rows & (rows - 1) == 0
        and channels == LANES
        and rows * (width // C) == LANES
        and LANES % total == 0
        and width == C * C == 8 * LANES
        and rows * CORES == 8
        and (rows * size // CORES) * (LANES // C) == LANES
    )


def local(left, right, depth, w_out, bias, pair_cot):
    if gathers(left, pair_cot, w_out):
        return gathered(left, right, depth, w_out, bias, pair_cot)
    return reduced(left, right, depth, w_out, bias, pair_cot)


def reduced(left, right, depth, w_out, bias, pair_cot):
    rows = left.shape[0]
    width = left.shape[1]
    alignment = width // C
    total = pair_cot.shape[1]
    channels = w_out.shape[1]
    row_ids = jnp.arange(alignment, dtype=jnp.int32)
    own_mask = (row_ids[None, :] < depth[:, None]).astype(jnp.bfloat16)
    own_left = left.reshape(rows, alignment, C) * own_mask[:, :, None]
    w_back = w_out.T
    pair_cols = lax.all_to_all(pair_cot, "pi", split_axis=1, concat_axis=0, tiled=True)
    init = (
        jnp.zeros((rows, total, channels), jnp.bfloat16),
        jnp.zeros((rows, width), jnp.float32),
        jnp.zeros((C * C, channels), jnp.float32),
        jnp.zeros((channels,), jnp.float32),
    )
    carry = init
    start = jnp.int32(0)
    right_piece = lax.all_gather(right, "pi", axis=0, tiled=True)
    depth_piece = lax.all_gather(depth, "pi", axis=0, tiled=True)
    length = right_piece.shape[0]
    block = math.gcd(length, 256)
    for offset in range(0, length, block):
        begin = start + offset
        depth_block = depth_piece[offset : offset + block]
        mask_block = (row_ids[None, :] < depth_block[:, None]).astype(jnp.bfloat16)
        right_block = (
            right_piece[offset : offset + block].reshape(block, alignment, C)
            * mask_block[:, :, None]
        )
        count = epsilon + jnp.minimum(depth[:, None], depth_block[None, :]).astype(jnp.float32)
        outer = jnp.einsum(
            "isc,jsd->ijcd", own_left, right_block, preferred_element_type=jnp.float32
        )
        outer = (outer / count[:, :, None, None]).reshape(rows, block, C * C).astype(jnp.bfloat16)
        update = (jnp.dot(outer, w_out, preferred_element_type=jnp.float32) + bias).astype(
            jnp.bfloat16
        )
        cot_block = lax.dynamic_slice_in_dim(pair_cot, begin, block, 1)
        pair_out = lax.dynamic_update_slice(carry[0], update, (0, begin, 0))
        weight_acc = carry[2] + jnp.dot(
            outer.reshape(-1, C * C).T,
            cot_block.reshape(-1, channels),
            preferred_element_type=jnp.float32,
        )
        bias_acc = carry[3] + jnp.sum(cot_block, axis=(0, 1), dtype=jnp.float32)
        grad_pair = (
            jnp.dot(cot_block, w_back, preferred_element_type=jnp.float32) / count[:, :, None]
        )
        grad_pair = grad_pair.astype(jnp.bfloat16).reshape(rows, block, C, C)
        left_acc = carry[1] + jnp.einsum(
            "ijcd,jsd->isc", grad_pair, right_block, preferred_element_type=jnp.float32
        ).reshape(rows, width)
        carry = (pair_out, left_acc, weight_acc, bias_acc)
    pair_update = carry[0]
    left_acc = carry[1]
    accum = jnp.zeros((rows, width), jnp.float32)
    start = jnp.int32(0)
    left_piece = lax.all_gather(left, "pi", axis=0, tiled=True)
    depth_piece = lax.all_gather(depth, "pi", axis=0, tiled=True)
    length = left_piece.shape[0]
    block = math.gcd(length, 256)
    for offset in range(0, length, block):
        begin = start + offset
        depth_block = depth_piece[offset : offset + block]
        mask_block = (row_ids[None, :] < depth_block[:, None]).astype(jnp.bfloat16)
        left_block = (
            left_piece[offset : offset + block].reshape(block, alignment, C)
            * mask_block[:, :, None]
        )
        count = epsilon + jnp.minimum(depth_block[:, None], depth[None, :]).astype(jnp.float32)
        cot_block = lax.dynamic_slice_in_dim(pair_cols, begin, block, 0)
        grad_pair = (
            jnp.dot(cot_block, w_back, preferred_element_type=jnp.float32) / count[:, :, None]
        )
        grad_pair = grad_pair.astype(jnp.bfloat16).reshape(block, rows, C, C)
        accum = accum + jnp.einsum(
            "ijcd,isc->jsd", grad_pair, left_block, preferred_element_type=jnp.float32
        ).reshape(rows, width)
    grad_w, grad_bias = lax.psum((carry[2], carry[3]), "pi")
    grad_left = (left_acc.reshape(rows, alignment, C) * own_mask[:, :, None]).reshape(rows, width)
    grad_right = (accum.reshape(rows, alignment, C) * own_mask[:, :, None]).reshape(rows, width)
    return (pair_update, grad_left, grad_right, grad_w, grad_bias)


def solution(mesh):
    placed = (
        P(("grp", "pi"), None),
        P(("grp", "pi"), None),
        P(("grp", "pi")),
        P(),
        P(),
        P(("grp", "pi"), None, None),
    )
    return jax.shard_map(
        local,
        mesh=mesh,
        in_specs=placed,
        out_specs=(
            P(("grp", "pi"), None, None),
            P(("grp", "pi"), None),
            P(("grp", "pi"), None),
            P("grp", None),
            P("grp"),
        ),
        check_vma=False,
    )
```

```python
import functools
import math

import jax
import jax.numpy as jnp
from jax import lax
from jax.experimental import pallas as pl
from jax.experimental.pallas import tpu as pltpu
from jax.sharding import PartitionSpec as P

C = 32
LANES = 128
CORES = 2
SMALL = 8 * 2**20
LARGE = 24 * 2**20


epsilon = 0.001

F32 = jnp.float32
BF16 = jnp.bfloat16


def iota(shape, dim):
    return lax.broadcasted_iota(jnp.int32, shape, dim)


def dot(x, y, contract_x, contract_y):
    return lax.dot_general(
        x, y, (((contract_x,), (contract_y,)), ((), ())), preferred_element_type=F32
    )


def views(refs, used):
    return [
        ref.at[k * used : (k + 1) * used, :]
        for ref in refs
        for k in range(ref.shape[0] // used)
    ]


def pack_kernel(
    left_ref, right_ref, cot_ref, depth_ref, bias_ref, w_ref,
    payload_ref, bias_out_ref, w_out_ref,
    left_here, right_here, depth_here, sems,
):
    rows, width = left_here.shape
    pairs = cot_ref.shape[0]
    total = pairs // rows
    alignment = width // C
    tiles = width // LANES
    group = LANES // C
    chip_rows = CORES * rows
    ends = (
        (depth_ref, depth_here),
        (left_ref, left_here),
        (right_ref, right_here),
        (cot_ref, payload_ref.at[:pairs, :]),
        (bias_ref, bias_out_ref),
        (w_ref, w_out_ref),
    )
    copies = [pltpu.make_async_copy(*pair, sems.at[k]) for k, pair in enumerate(ends)]
    for copy in copies:
        copy.start()
    for copy in copies[:3]:
        copy.wait()
    left = left_here[...].astype(F32)
    flat = jnp.concatenate([left[:, t * LANES : (t + 1) * LANES] for t in range(tiles)], 0)
    flat = flat.astype(BF16)
    row = iota((tiles * rows, LANES), 0)
    lane = iota((tiles * rows, LANES), 1)
    target = lax.rem(row, rows) * alignment + row // rows * group
    turned = jnp.zeros((C, LANES), F32)
    for q in range(group):
        place = (lane == target + q).astype(F32).astype(BF16)
        turned = turned + dot(flat, place, 0, 0)[q * C : (q + 1) * C, :]
    lane = iota((C, LANES), 1)
    depth = jnp.zeros((C, LANES), jnp.int32)
    for i in range(rows):
        depth = jnp.where(lane // alignment == i, depth_here[i], depth)
    turned = jnp.where(lax.rem(lane, alignment) < depth, turned, 0.0)
    payload_ref[pairs : pairs + C, :] = turned.astype(BF16)
    own = right_here[...].astype(F32)
    parts = [own[:, t * LANES : (t + 1) * LANES] for t in range(tiles)]
    row = iota((8, LANES), 0)
    depth = jnp.zeros((8, LANES), jnp.int32)
    for i in range(rows):
        depth = jnp.where(row == i, depth_here[i], depth)
    parts.append(depth.astype(F32))
    lane = row * LANES + iota((8, LANES), 1)
    depth = jnp.zeros((8, LANES), jnp.int32)
    for i in range(rows):
        depth = jnp.where(lane // total == i, depth_here[i], depth)
    parts.append(depth.astype(F32))
    payload_ref[pairs + C :, :] = jnp.concatenate(parts, 0).astype(BF16)
    for copy in copies[3:]:
        copy.wait()


def collect_kernel(used, begin, *refs):
    piece, out_ref = views(refs[:-1], used), refs[-1]
    tail = [ref[begin:, :].astype(F32) for ref in piece]
    tiles = C * C // LANES + 1
    half = out_ref.shape[0] // tiles
    rows = half // len(piece)
    for tile in range(tiles):
        part = jnp.concatenate([x[tile * rows : (tile + 1) * rows] for x in tail], 0)
        out_ref[tile * half : (tile + 1) * half, :] = part.astype(BF16)


def sum_kernel(
    rows, own_ref, other_ref, update_here, left_here,
    update_ref, left_ref, w_ref, right_ref, bias_ref, w_here, right_here, bias_here, sems,
):
    copies = [
        pltpu.make_async_copy(update_here, update_ref, sems.at[0]),
        pltpu.make_async_copy(left_here, left_ref, sems.at[1]),
        pltpu.make_async_copy(right_here, right_ref, sems.at[2]),
        pltpu.make_async_copy(bias_here, bias_ref, sems.at[3]),
    ]
    copies[0].start()
    copies[1].start()
    wide = w_ref.shape[0]
    core = lax.rem(lax.axis_index("pi"), CORES)
    tiles = right_ref.shape[1] // LANES
    begin = pl.multiple_of(wide + core * rows * tiles, 8)
    part = own_ref[pl.ds(begin, rows * tiles), :] + other_ref[pl.ds(begin, rows * tiles), :]
    for row in range(rows):
        for tile in range(tiles):
            at = row * tiles + tile
            right_here[row : row + 1, tile * LANES : (tile + 1) * LANES] = part[at : at + 1, :]
    last = wide + CORES * rows * tiles
    bias_here[...] = own_ref[last : last + 1, :] + other_ref[last : last + 1, :]
    copies[2].start()
    copies[3].start()
    count = sems.shape[0] - 4
    for k in range(count):
        some = slice(k * wide // count, (k + 1) * wide // count)
        w_here[some, :] = own_ref[some, :] + other_ref[some, :]
        copies.append(pltpu.make_async_copy(w_here.at[some], w_ref.at[some], sems.at[4 + k]))
        copies[-1].start()
    for copy in copies:
        copy.wait()


def right_kernel(sizes, *refs):
    rows, total, pieces, alignment, used, arrays = sizes
    some = 8
    piece = views(refs[:arrays], used)
    w_ref, depth_ref, out_ref, w_swap_ref = refs[arrays : arrays + 4]
    left_wide, window, picked, weights, g_right, stage, depths, w_wide = refs[arrays + 4 :]
    chip_rows = CORES * rows
    pairs = rows * total
    tiles = C * C // LANES
    group = LANES // C
    me = lax.axis_index("pi")
    chip = me // CORES
    at_depth = pairs + C + tiles * rows

    w_wide[...] = w_ref[...].astype(F32)
    for d in range(C):
        w_swap_ref[d * C : (d + 1) * C, :] = w_wide[pl.ds(d, C, stride=C), :].astype(BF16)
    for m in range(pieces):
        left_wide[m * C : (m + 1) * C, :] = piece[m][pairs : pairs + C, :].astype(F32)
    tail = [ref[at_depth : at_depth + 16, :].astype(F32)[:rows] for ref in piece]
    other = jnp.broadcast_to(depth_ref[...].astype(F32), (rows, rows))
    other = jnp.where(iota((rows, rows), 0) == iota((rows, rows), 1), other, 0.0)
    other = jnp.broadcast_to(jnp.sum(other, axis=1, keepdims=True), (rows, LANES))
    depths[...] = jnp.concatenate([tail[0], other, jnp.zeros((8, LANES), F32)], 0)
    half = lax.rem(chip, 16 // chip_rows)
    for m in range(pieces):
        for i in range(rows):
            begin = i * total + chip * chip_rows - half * chip_rows
            two = piece[m][pl.ds(pl.multiple_of(begin, 16), 16), :].astype(F32)
            one = two[:chip_rows]
            for k in range(1, 16 // chip_rows):
                one = jnp.where(half == k, two[k * chip_rows : (k + 1) * chip_rows], one)
            at = (i * pieces + m) * chip_rows
            window[at : at + chip_rows, :] = one
    mine = rows * pieces
    for j in range(chip_rows):
        picked[j * mine : (j + 1) * mine, :] = window[
            pl.ds(j, mine, stride=chip_rows), :
        ].astype(BF16)
    count_lanes = chip_rows * mine
    lane = lax.rem(iota((mine, count_lanes), 1), mine)
    from_i = iota((mine, count_lanes), 0) == lax.rem(lane, pieces) * rows + lane // pieces
    lane = iota((16, count_lanes), 1) // mine
    from_j = iota((16, count_lanes), 0) == lax.bitwise_xor(lane, lax.rem(me, CORES) * rows)
    depth_i = jnp.concatenate(tail, 0).astype(BF16)
    depth_i = dot(depth_i, from_i.astype(F32).astype(BF16), 0, 0)[:8, :]
    depth_j = dot(depths[...].astype(BF16), from_j.astype(F32).astype(BF16), 0, 0)[:8, :]
    inverse_right = (1.0 / (epsilon + jnp.minimum(depth_i, depth_j)))[:1, :]
    for c in range(C):
        if c % some == 0:
            g = dot(w_ref[c * C : (c + some) * C, :], picked[...], 1, 1)
            g = (g * inverse_right).astype(BF16)
        for k in range(count_lanes // LANES):
            g_right[k * C : (k + 1) * C, c * LANES : (c + 1) * LANES] = g[
                c % some * C : (c % some + 1) * C, k * LANES : (k + 1) * LANES
            ]
        feature = left_wide[pl.ds(c, pieces, stride=C), :]
        turns = [feature] + [pltpu.roll(feature, k * alignment, 1) for k in range(1, rows)]
        block_of = iota((pieces, LANES), 1) // alignment
        for j in range(group):
            both = jnp.concatenate(
                [jnp.where(block_of == j, turns[(j - i) % rows], 0.0) for i in range(rows)], 0
            )
            at = c * LANES + j * mine
            weights[at : at + mine, :] = both.astype(BF16)
    right_grad = dot(g_right[...], weights[...], 1, 0)
    in_tile = iota((8, LANES), 1) // C
    row_of = (iota((8, LANES), 0) * group + in_tile).astype(F32)
    for k in range(count_lanes // LANES):
        part = right_grad[k * C : (k + 1) * C, :]
        stage[...] = jnp.concatenate([part] * group, 0).T
        for j in range(group):
            flat = jnp.zeros((8, LANES), F32)
            for q in range(group):
                flat = jnp.where(
                    in_tile == q, stage[pl.ds(j * alignment + q, tiles, stride=group), :], flat
                )
            residue = lax.bitwise_xor(k * group + j, lax.rem(me, CORES) * rows)
            depth = depths[pl.ds(residue, 1), :]
            at = (k * group + j) * tiles
            out_ref[at : at + tiles, :] = jnp.where(row_of < depth, flat, 0.0)


def main_kernel(sizes, *refs):
    rows, total, pieces, used, arrays, route = sizes
    piece = views(refs[:arrays], used)
    own_ref, other_ref, right_ref = refs[arrays : arrays + 3]
    partial_ref, spread, outer_own, inverse_own = refs[arrays + 3 : arrays + 7]
    turned, left_all, cots, inverse, outer = refs[arrays + 7 :]
    pairs = rows * total
    tiles = C * C // LANES
    per_tile = LANES // total
    me = lax.axis_index("pi")
    at_pairs = pairs + C + tiles * rows

    for m in range(pieces):
        left_all[m * C : (m + 1) * C, :] = piece[m][pairs : pairs + C, :]
        cots[m * pairs : (m + 1) * pairs, :] = piece[m][:pairs, :]
    half = total // CORES
    row = iota((total, LANES), 0)
    core = lax.rem(me, CORES)
    step = jnp.zeros((total, LANES), jnp.int32)
    for m, offset in enumerate(offsets(route)):
        for k in range(CORES):
            at = row // rows == k * pieces + m
            step = jnp.where(at, jnp.where(core == k, offset[0], offset[1]) + k, step)
    source = lax.bitwise_xor(step, me) * rows + lax.rem(row, rows)
    place = (source == lax.rem(iota((total, LANES), 1), total)).astype(F32).astype(BF16)
    both = [
        jnp.concatenate([ref[t * half : (t + 1) * half, :] for ref in (own_ref, other_ref)], 0)
        for t in range(tiles + 1)
    ]
    for tile in range(tiles):
        turned[tile * LANES : (tile + 1) * LANES, :] = dot(both[tile], place, 0, 0)
    depth_lane = dot(both[tiles], place, 0, 0)

    for m in range(pieces):
        block = piece[m][at_pairs : at_pairs + 16, :].astype(F32)
        for tile in range(pairs // LANES):
            least = jnp.minimum(block[8 + tile : 9 + tile, :], depth_lane[:1, :])
            inverse[m : m + 1, tile * LANES : (tile + 1) * LANES] = 1.0 / (epsilon + least)

    alignment = spread.shape[0] // rows
    alive = iota((alignment, LANES), 0).astype(F32) < depth_lane[:alignment, :]
    part_of = iota((alignment, LANES), 1) // total
    keep = [jnp.where(alive & (part_of == k), 1.0, 0.0).astype(F32) for k in range(per_tile)]
    nothing = jnp.zeros((alignment, LANES), BF16)
    for d in range(C):
        block = turned[pl.ds(d, alignment, stride=C), :]
        kept = [(block * keep[k]).astype(BF16) for k in range(per_tile)]
        for i in range(rows):
            for tile in range(pairs // LANES):
                spread[
                    i * alignment : (i + 1) * alignment,
                    d * pairs + tile * LANES : d * pairs + (tile + 1) * LANES,
                ] = kept[i % per_tile] if i // per_tile == tile else nothing

    chunk = 8
    for d in range(C):
        o = dot(left_all[...], spread[:, d * pairs : (d + 1) * pairs], 1, 0)
        for m in range(pieces):
            outer[d * C : (d + 1) * C, m * pairs : (m + 1) * pairs] = (
                o[m * C : (m + 1) * C, :] * inverse[m : m + 1, :]
            ).astype(BF16)
        if d % chunk == chunk - 1:
            first = d + 1 - chunk
            some = slice(first * C, (d + 1) * C)
            outer_own[some, :] = outer[some, :pairs]
            grad = dot(outer[some, :], cots[...], 1, 0)
            for k in range(chunk):
                partial_ref[pl.ds(first + k, C, stride=C), :] = grad[k * C : (k + 1) * C, :]
    wide = C * C
    last = wide + right_ref.shape[0]
    partial_ref[wide:last, :] = right_ref[...]
    partial_ref[last : last + 8, :] = dot(
        jnp.ones((8, pieces * pairs), BF16), cots[...], 1, 0
    )
    inverse_own[...] = inverse[...]


def own_kernel(
    rows, spread, outer_own, inverse_own, payload_ref, w_swap_ref, bias_ref,
    update_ref, left_ref, g_left, stage,
):
    some = 8
    pairs = update_ref.shape[0]
    alignment = spread.shape[0] // rows
    tiles = left_ref.shape[1] // LANES
    group = LANES // C
    update = dot(outer_own[...], w_swap_ref[...], 0, 0)
    update_ref[...] = (update + bias_ref[...]).astype(BF16)
    for d in range(C):
        if d % some == 0:
            g = dot(w_swap_ref[d * C : (d + some) * C, :], payload_ref[:pairs, :], 1, 1)
            g = (g * inverse_own[:1, :]).astype(BF16)
        g_left[:, d * pairs : (d + 1) * pairs] = g[d % some * C : (d % some + 1) * C, :]
    left_grad = dot(spread[...], g_left[...], 1, 1)
    stage[...] = jnp.concatenate([left_grad] * group, 1)
    in_tile = iota((8, LANES), 1) // C
    row_of = (iota((8, LANES), 0) * group + in_tile).astype(F32)
    at_depth = pairs + C + tiles * rows
    depth = payload_ref[at_depth : at_depth + 16, :].astype(F32)
    for i in range(rows):
        flat = jnp.zeros((8, LANES), F32)
        for q in range(group):
            flat = jnp.where(
                in_tile == q, stage[pl.ds(i * alignment + q, tiles, stride=group), :], flat
            )
        flat = jnp.where(row_of < depth[i : i + 1, :], flat, 0.0)
        for tile in range(tiles):
            left_ref[i : i + 1, tile * LANES : (tile + 1) * LANES] = flat[tile : tile + 1, :]


def swap(x, masks, size):
    return lax.ppermute(x, "pi", [(i, i ^ masks[i % CORES]) for i in range(size)])


def route_of(size):
    near, middle, far = CORES, size // 4, size // 2
    if near * 2 == middle:
        return (
            ((0,), (far + middle + near,) * CORES),
            ((0,), (far + middle,) * CORES),
            ((0,), (near,) * CORES),
            ((3,), (middle,) * CORES),
            ((0,), (middle,) * CORES),
            ((0,), (far,) * CORES),
            ((6,), (near,) * CORES),
        )
    return tuple(((0,), (offset,) * CORES) for offset in range(CORES, size, CORES))


def offsets(route):
    found = [(0,) * CORES]
    for sources, hops in route:
        found += [tuple(a ^ b for a, b in zip(found[k], hops)) for k in sources]
    return found


def gathered(left, right, depth, w_out, bias, pair_cot):
    rows, width = left.shape
    alignment = width // C
    total, channels = pair_cot.shape[1:]
    size = lax.axis_size("pi")
    pieces = size // CORES
    pairs = rows * total
    chip_rows = CORES * rows
    tiles = width // LANES
    used = pairs + C + tiles * rows + 16
    hbm = pl.BlockSpec(memory_space=pltpu.HBM)
    vmem = pl.BlockSpec(memory_space=pltpu.VMEM)
    depth_other = swap(depth, (1, 1), size)
    given = (
        left, right, pair_cot.reshape(pairs, channels), depth, bias.reshape(1, channels), w_out,
    )
    payload, bias_row, w_here = pl.pallas_call(
        pack_kernel,
        out_shape=(
            pltpu.VMEM((used, LANES), BF16),
            pltpu.VMEM((1, channels), F32),
            pltpu.VMEM(w_out.shape, BF16),
        ),
        in_specs=[hbm] * 6,
        out_specs=(vmem, vmem, vmem),
        scratch_shapes=[
            pltpu.VMEM(left.shape, BF16),
            pltpu.VMEM(right.shape, BF16),
            pltpu.SMEM(depth.shape, jnp.int32),
            pltpu.SemaphoreType.DMA((6,)),
        ],
        compiler_params=pltpu.CompilerParams(vmem_limit_bytes=SMALL),
        cost_estimate=pl.CostEstimate(flops=10**9, bytes_accessed=2**20, transcendentals=0),
    )(*[pltpu.with_memory_space_constraint(x, pltpu.HBM) for x in given])
    arrived = [payload]
    place = {0: payload}
    route = route_of(size)
    for sources, hops in route:
        message = [place[k] for k in sources]
        message = swap(jnp.concatenate(message, 0) if len(message) > 1 else message[0], hops, size)
        if len(sources) == 1:
            place[sum(x.shape[0] for x in arrived) // used] = message
        arrived.append(message)
    mine = pl.pallas_call(
        functools.partial(collect_kernel, used, pairs + C),
        out_shape=pltpu.VMEM((total // CORES * (tiles + 1), LANES), BF16),
        compiler_params=pltpu.CompilerParams(vmem_limit_bytes=SMALL),
    )(*arrived)
    theirs = swap(mine, (1, 1), size)
    count_lanes = chip_rows * rows * pieces
    right_partial, w_swap = pl.pallas_call(
        functools.partial(right_kernel, (rows, total, pieces, alignment, used, len(arrived))),
        out_shape=(pltpu.VMEM((chip_rows * tiles, LANES), F32), pltpu.VMEM(w_out.shape, BF16)),
        scratch_shapes=[
            pltpu.VMEM((pieces * C, LANES), F32),
            pltpu.VMEM((count_lanes, channels), F32),
            pltpu.VMEM((count_lanes, channels), BF16),
            pltpu.VMEM((C * LANES, LANES), BF16),
            pltpu.VMEM((count_lanes // LANES * C, C * LANES), BF16),
            pltpu.VMEM((LANES, LANES), F32),
            pltpu.VMEM((16, LANES), F32),
            pltpu.VMEM(w_out.shape, F32),
        ],
        compiler_params=pltpu.CompilerParams(vmem_limit_bytes=LARGE),
        cost_estimate=pl.CostEstimate(flops=10**9, bytes_accessed=2**20, transcendentals=0),
    )(*arrived, w_here, depth_other.reshape(1, rows))
    partial, spread, outer_own, inverse_own = pl.pallas_call(
        functools.partial(main_kernel, (rows, total, pieces, used, len(arrived), route)),
        out_shape=(
            pltpu.VMEM((C * C + chip_rows * tiles + 8, LANES), F32),
            pltpu.VMEM((rows * alignment, C * pairs), BF16),
            pltpu.VMEM((C * C, pairs), BF16),
            pltpu.VMEM((pieces, pairs), F32),
        ),
        scratch_shapes=[
            pltpu.VMEM((width, LANES), F32),
            pltpu.VMEM((pieces * C, LANES), BF16),
            pltpu.VMEM((pieces * pairs, channels), BF16),
            pltpu.VMEM((pieces, pairs), F32),
            pltpu.VMEM((C * C, pieces * pairs), BF16),
        ],
        compiler_params=pltpu.CompilerParams(vmem_limit_bytes=LARGE),
    )(*arrived, mine, theirs, right_partial)
    other = swap(partial, (1, 1), size)
    update, grad_left = pl.pallas_call(
        functools.partial(own_kernel, rows),
        out_shape=(pltpu.VMEM((pairs, channels), BF16), pltpu.VMEM((rows, width), F32)),
        scratch_shapes=[
            pltpu.VMEM((C, C * pairs), BF16),
            pltpu.VMEM((LANES, LANES), F32),
        ],
        compiler_params=pltpu.CompilerParams(vmem_limit_bytes=LARGE),
        cost_estimate=pl.CostEstimate(
            flops=8 * pairs * C * C * channels, bytes_accessed=4 * 2**20, transcendentals=0
        ),
    )(spread, outer_own, inverse_own, payload, w_swap, bias_row)
    update, grad_left, grad_w, grad_right, grad_bias = pl.pallas_call(
        functools.partial(sum_kernel, rows),
        out_shape=(
            jax.ShapeDtypeStruct((pairs, channels), BF16),
            jax.ShapeDtypeStruct((rows, width), F32),
            jax.ShapeDtypeStruct((C * C, channels), F32),
            jax.ShapeDtypeStruct((rows, width), F32),
            jax.ShapeDtypeStruct((1, channels), F32),
        ),
        out_specs=(hbm,) * 5,
        scratch_shapes=[
            pltpu.VMEM((C * C, channels), F32),
            pltpu.VMEM((rows, width), F32),
            pltpu.VMEM((1, channels), F32),
            pltpu.SemaphoreType.DMA((8,)),
        ],
        compiler_params=pltpu.CompilerParams(vmem_limit_bytes=SMALL),
    )(partial, other, update, grad_left)
    return (
        update.reshape(rows, total, channels),
        grad_left,
        grad_right,
        grad_w,
        grad_bias.reshape(channels),
    )


def gathers(left, pair_cot, w_out):
    rows, width = left.shape
    total, channels = pair_cot.shape[1:]
    size = lax.axis_size("pi")
    gather_bytes = size * pair_cot.size * 2
    reduce_bytes = 2 * w_out.size * 4
    return (
        gather_bytes <= reduce_bytes
        and size >= 2 * CORES
        and size & (size - 1) == 0
        and rows & (rows - 1) == 0
        and channels == LANES
        and rows * (width // C) == LANES
        and LANES % total == 0
        and width == C * C == 8 * LANES
        and rows * CORES == 8
        and (rows * size // CORES) * (LANES // C) == LANES
    )


def local(left, right, depth, w_out, bias, pair_cot):
    if gathers(left, pair_cot, w_out):
        return gathered(left, right, depth, w_out, bias, pair_cot)
    return reduced(left, right, depth, w_out, bias, pair_cot)


def reduced(left, right, depth, w_out, bias, pair_cot):
    rows = left.shape[0]
    width = left.shape[1]
    alignment = width // C
    total = pair_cot.shape[1]
    channels = w_out.shape[1]
    row_ids = jnp.arange(alignment, dtype=jnp.int32)
    own_mask = (row_ids[None, :] < depth[:, None]).astype(jnp.bfloat16)
    own_left = left.reshape(rows, alignment, C) * own_mask[:, :, None]
    w_back = w_out.T
    pair_cols = lax.all_to_all(pair_cot, "pi", split_axis=1, concat_axis=0, tiled=True)
    init = (
        jnp.zeros((rows, total, channels), jnp.bfloat16),
        jnp.zeros((rows, width), jnp.float32),
        jnp.zeros((C * C, channels), jnp.float32),
        jnp.zeros((channels,), jnp.float32),
    )
    carry = init
    start = jnp.int32(0)
    right_piece = lax.all_gather(right, "pi", axis=0, tiled=True)
    depth_piece = lax.all_gather(depth, "pi", axis=0, tiled=True)
    length = right_piece.shape[0]
    block = math.gcd(length, 256)
    for offset in range(0, length, block):
        begin = start + offset
        depth_block = depth_piece[offset : offset + block]
        mask_block = (row_ids[None, :] < depth_block[:, None]).astype(jnp.bfloat16)
        right_block = (
            right_piece[offset : offset + block].reshape(block, alignment, C)
            * mask_block[:, :, None]
        )
        count = epsilon + jnp.minimum(depth[:, None], depth_block[None, :]).astype(jnp.float32)
        outer = jnp.einsum(
            "isc,jsd->ijcd", own_left, right_block, preferred_element_type=jnp.float32
        )
        outer = (outer / count[:, :, None, None]).reshape(rows, block, C * C).astype(jnp.bfloat16)
        update = (jnp.dot(outer, w_out, preferred_element_type=jnp.float32) + bias).astype(
            jnp.bfloat16
        )
        cot_block = lax.dynamic_slice_in_dim(pair_cot, begin, block, 1)
        pair_out = lax.dynamic_update_slice(carry[0], update, (0, begin, 0))
        weight_acc = carry[2] + jnp.dot(
            outer.reshape(-1, C * C).T,
            cot_block.reshape(-1, channels),
            preferred_element_type=jnp.float32,
        )
        bias_acc = carry[3] + jnp.sum(cot_block, axis=(0, 1), dtype=jnp.float32)
        grad_pair = (
            jnp.dot(cot_block, w_back, preferred_element_type=jnp.float32) / count[:, :, None]
        )
        grad_pair = grad_pair.astype(jnp.bfloat16).reshape(rows, block, C, C)
        left_acc = carry[1] + jnp.einsum(
            "ijcd,jsd->isc", grad_pair, right_block, preferred_element_type=jnp.float32
        ).reshape(rows, width)
        carry = (pair_out, left_acc, weight_acc, bias_acc)
    pair_update = carry[0]
    left_acc = carry[1]
    accum = jnp.zeros((rows, width), jnp.float32)
    start = jnp.int32(0)
    left_piece = lax.all_gather(left, "pi", axis=0, tiled=True)
    depth_piece = lax.all_gather(depth, "pi", axis=0, tiled=True)
    length = left_piece.shape[0]
    block = math.gcd(length, 256)
    for offset in range(0, length, block):
        begin = start + offset
        depth_block = depth_piece[offset : offset + block]
        mask_block = (row_ids[None, :] < depth_block[:, None]).astype(jnp.bfloat16)
        left_block = (
            left_piece[offset : offset + block].reshape(block, alignment, C)
            * mask_block[:, :, None]
        )
        count = epsilon + jnp.minimum(depth_block[:, None], depth[None, :]).astype(jnp.float32)
        cot_block = lax.dynamic_slice_in_dim(pair_cols, begin, block, 0)
        grad_pair = (
            jnp.dot(cot_block, w_back, preferred_element_type=jnp.float32) / count[:, :, None]
        )
        grad_pair = grad_pair.astype(jnp.bfloat16).reshape(block, rows, C, C)
        accum = accum + jnp.einsum(
            "ijcd,isc->jsd", grad_pair, left_block, preferred_element_type=jnp.float32
        ).reshape(rows, width)
    grad_w, grad_bias = lax.psum((carry[2], carry[3]), "pi")
    grad_left = (left_acc.reshape(rows, alignment, C) * own_mask[:, :, None]).reshape(rows, width)
    grad_right = (accum.reshape(rows, alignment, C) * own_mask[:, :, None]).reshape(rows, width)
    return (pair_update, grad_left, grad_right, grad_w, grad_bias)


def solution(mesh):
    placed = (
        P(("grp", "pi"), None),
        P(("grp", "pi"), None),
        P(("grp", "pi")),
        P(),
        P(),
        P(("grp", "pi"), None, None),
    )
    return jax.shard_map(
        local,
        mesh=mesh,
        in_specs=placed,
        out_specs=(
            P(("grp", "pi"), None, None),
            P(("grp", "pi"), None),
            P(("grp", "pi"), None),
            P("grp", None),
            P("grp"),
        ),
        check_vma=False,
    )
```

```python
import functools
import math

import jax
import jax.numpy as jnp
from jax import lax
from jax.experimental import pallas as pl
from jax.experimental.pallas import tpu as pltpu
from jax.sharding import PartitionSpec as P

C = 32
LANES = 128
CORES = 2
SMALL = 8 * 2**20
LARGE = 24 * 2**20


epsilon = 0.001

F32 = jnp.float32
BF16 = jnp.bfloat16


def iota(shape, dim):
    return lax.broadcasted_iota(jnp.int32, shape, dim)


def dot(x, y, contract_x, contract_y):
    return lax.dot_general(
        x, y, (((contract_x,), (contract_y,)), ((), ())), preferred_element_type=F32
    )


def views(refs, used):
    return [
        ref.at[k * used : (k + 1) * used, :]
        for ref in refs
        for k in range(ref.shape[0] // used)
    ]


def pack_kernel(
    left_ref, right_ref, cot_ref, depth_ref, bias_ref, w_ref,
    payload_ref, bias_out_ref, w_out_ref,
    left_here, right_here, depth_here, sems,
):
    rows, width = left_here.shape
    pairs = cot_ref.shape[0]
    total = pairs // rows
    alignment = width // C
    tiles = width // LANES
    group = LANES // C
    chip_rows = CORES * rows
    ends = (
        (depth_ref, depth_here),
        (left_ref, left_here),
        (right_ref, right_here),
        (cot_ref, payload_ref.at[:pairs, :]),
        (bias_ref, bias_out_ref),
        (w_ref, w_out_ref),
    )
    copies = [pltpu.make_async_copy(*pair, sems.at[k]) for k, pair in enumerate(ends)]
    for copy in copies:
        copy.start()
    row = iota((tiles * rows, group * LANES), 0)
    lane = iota((tiles * rows, group * LANES), 1)
    target = lax.rem(row, rows) * alignment + row // rows * group + lane // LANES
    place = (lax.rem(lane, LANES) == target).astype(F32).astype(BF16)
    for copy in copies[:3]:
        copy.wait()
    left = left_here[...].astype(F32)
    flat = jnp.concatenate([left[:, t * LANES : (t + 1) * LANES] for t in range(tiles)], 0)
    flat = flat.astype(BF16)
    spots = dot(flat, place, 0, 0)
    turned = jnp.zeros((C, LANES), F32)
    for q in range(group):
        turned = turned + spots[q * C : (q + 1) * C, q * LANES : (q + 1) * LANES]
    lane = iota((C, LANES), 1)
    depth = jnp.zeros((C, LANES), jnp.int32)
    for i in range(rows):
        depth = jnp.where(lane // alignment == i, depth_here[i], depth)
    turned = jnp.where(lax.rem(lane, alignment) < depth, turned, 0.0)
    payload_ref[pairs : pairs + C, :] = turned.astype(BF16)
    own = right_here[...].astype(F32)
    parts = [own[:, t * LANES : (t + 1) * LANES] for t in range(tiles)]
    row = iota((8, LANES), 0)
    depth = jnp.zeros((8, LANES), jnp.int32)
    for i in range(rows):
        depth = jnp.where(row == i, depth_here[i], depth)
    parts.append(depth.astype(F32))
    lane = row * LANES + iota((8, LANES), 1)
    depth = jnp.zeros((8, LANES), jnp.int32)
    for i in range(rows):
        depth = jnp.where(lane // total == i, depth_here[i], depth)
    parts.append(depth.astype(F32))
    payload_ref[pairs + C :, :] = jnp.concatenate(parts, 0).astype(BF16)
    for copy in copies[3:]:
        copy.wait()


def collect_kernel(used, begin, *refs):
    piece, out_ref = views(refs[:-1], used), refs[-1]
    tail = [ref[begin:, :].astype(F32) for ref in piece]
    tiles = C * C // LANES + 1
    half = out_ref.shape[0] // tiles
    rows = half // len(piece)
    for tile in range(tiles):
        part = jnp.concatenate([x[tile * rows : (tile + 1) * rows] for x in tail], 0)
        out_ref[tile * half : (tile + 1) * half, :] = part.astype(BF16)


def sum_kernel(
    rows, own_ref, other_ref, update_here, left_here,
    update_ref, left_ref, w_ref, right_ref, bias_ref, w_here, right_here, bias_here, sems,
):
    copies = [
        pltpu.make_async_copy(update_here, update_ref, sems.at[0]),
        pltpu.make_async_copy(left_here, left_ref, sems.at[1]),
        pltpu.make_async_copy(right_here, right_ref, sems.at[2]),
        pltpu.make_async_copy(bias_here, bias_ref, sems.at[3]),
    ]
    copies[0].start()
    copies[1].start()
    wide = w_ref.shape[0]
    count = sems.shape[0] - 4
    for k in range(count):
        some = slice(k * wide // count, (k + 1) * wide // count)
        w_here[some, :] = own_ref[some, :] + other_ref[some, :]
        copies.append(pltpu.make_async_copy(w_here.at[some], w_ref.at[some], sems.at[4 + k]))
        copies[-1].start()
    core = lax.rem(lax.axis_index("pi"), CORES)
    tiles = right_ref.shape[1] // LANES
    begin = pl.multiple_of(wide + core * rows * tiles, 8)
    part = own_ref[pl.ds(begin, rows * tiles), :] + other_ref[pl.ds(begin, rows * tiles), :]
    for row in range(rows):
        for tile in range(tiles):
            at = row * tiles + tile
            right_here[row : row + 1, tile * LANES : (tile + 1) * LANES] = part[at : at + 1, :]
    last = wide + CORES * rows * tiles
    bias_here[...] = own_ref[last : last + 1, :] + other_ref[last : last + 1, :]
    copies[2].start()
    copies[3].start()
    for copy in copies:
        copy.wait()


def prepare_kernel(w_ref, early_ref, w_swap_ref, spread_ref, w_wide):
    w_wide[...] = w_ref[...].astype(F32)
    for d in range(C):
        w_swap_ref[d * C : (d + 1) * C, :] = w_wide[pl.ds(d, C, stride=C), :].astype(BF16)
    spread_ref[...] = jnp.zeros(spread_ref.shape, BF16)


def right_kernel(sizes, *refs):
    rows, total, pieces, alignment, used, arrays = sizes
    some = 8
    piece = views(refs[:arrays], used)
    w_ref, depth_ref, out_ref, cots, left_all = refs[arrays : arrays + 5]
    left_wide, window, picked, weights, g_right, stage, depths = refs[arrays + 5 :]
    chip_rows = CORES * rows
    pairs = rows * total
    tiles = C * C // LANES
    group = LANES // C
    me = lax.axis_index("pi")
    chip = me // CORES
    at_depth = pairs + C + tiles * rows

    for m in range(pieces):
        left_all[m * C : (m + 1) * C, :] = piece[m][pairs : pairs + C, :]
        cots[m * pairs : (m + 1) * pairs, :] = piece[m][:pairs, :]
        left_wide[m * C : (m + 1) * C, :] = piece[m][pairs : pairs + C, :].astype(F32)
    tail = [ref[at_depth : at_depth + 16, :].astype(F32)[:rows] for ref in piece]
    other = jnp.broadcast_to(depth_ref[...].astype(F32), (rows, rows))
    other = jnp.where(iota((rows, rows), 0) == iota((rows, rows), 1), other, 0.0)
    other = jnp.broadcast_to(jnp.sum(other, axis=1, keepdims=True), (rows, LANES))
    depths[...] = jnp.concatenate([tail[0], other, jnp.zeros((8, LANES), F32)], 0)
    half = lax.rem(chip, 16 // chip_rows)
    for m in range(pieces):
        for i in range(rows):
            begin = i * total + chip * chip_rows - half * chip_rows
            two = piece[m][pl.ds(pl.multiple_of(begin, 16), 16), :].astype(F32)
            one = two[:chip_rows]
            for k in range(1, 16 // chip_rows):
                one = jnp.where(half == k, two[k * chip_rows : (k + 1) * chip_rows], one)
            at = (i * pieces + m) * chip_rows
            window[at : at + chip_rows, :] = one
    mine = rows * pieces
    for j in range(chip_rows):
        picked[j * mine : (j + 1) * mine, :] = window[
            pl.ds(j, mine, stride=chip_rows), :
        ].astype(BF16)
    count_lanes = chip_rows * mine
    lane = lax.rem(iota((mine, count_lanes), 1), mine)
    from_i = iota((mine, count_lanes), 0) == lax.rem(lane, pieces) * rows + lane // pieces
    lane = iota((16, count_lanes), 1) // mine
    from_j = iota((16, count_lanes), 0) == lax.bitwise_xor(lane, lax.rem(me, CORES) * rows)
    depth_i = jnp.concatenate(tail, 0).astype(BF16)
    depth_i = dot(depth_i, from_i.astype(F32).astype(BF16), 0, 0)[:8, :]
    depth_j = dot(depths[...].astype(BF16), from_j.astype(F32).astype(BF16), 0, 0)[:8, :]
    inverse_right = (1.0 / (epsilon + jnp.minimum(depth_i, depth_j)))[:1, :]
    for c in range(C):
        if c % some == 0:
            g = dot(w_ref[c * C : (c + some) * C, :], picked[...], 1, 1)
            g = (g * inverse_right).astype(BF16)
        for k in range(count_lanes // LANES):
            g_right[k * C : (k + 1) * C, c * LANES : (c + 1) * LANES] = g[
                c % some * C : (c % some + 1) * C, k * LANES : (k + 1) * LANES
            ]
        feature = left_wide[pl.ds(c, pieces, stride=C), :]
        turns = [feature] + [pltpu.roll(feature, k * alignment, 1) for k in range(1, rows)]
        block_of = iota((pieces, LANES), 1) // alignment
        for j in range(group):
            both = jnp.concatenate(
                [jnp.where(block_of == j, turns[(j - i) % rows], 0.0) for i in range(rows)], 0
            )
            at = c * LANES + j * mine
            weights[at : at + mine, :] = both.astype(BF16)
    right_grad = dot(g_right[...], weights[...], 1, 0)
    in_tile = iota((8, LANES), 1) // C
    row_of = (iota((8, LANES), 0) * group + in_tile).astype(F32)
    for k in range(count_lanes // LANES):
        part = right_grad[k * C : (k + 1) * C, :]
        stage[...] = jnp.concatenate([part] * group, 0).T
        for j in range(group):
            flat = jnp.zeros((8, LANES), F32)
            for q in range(group):
                flat = jnp.where(
                    in_tile == q, stage[pl.ds(j * alignment + q, tiles, stride=group), :], flat
                )
            residue = lax.bitwise_xor(k * group + j, lax.rem(me, CORES) * rows)
            depth = depths[pl.ds(residue, 1), :]
            at = (k * group + j) * tiles
            out_ref[at : at + tiles, :] = jnp.where(row_of < depth, flat, 0.0)


def main_kernel(sizes, *refs):
    rows, total, pieces, used, arrays, route = sizes
    piece = views(refs[:arrays], used)
    own_ref, other_ref, right_ref, cots, left_all, _ = refs[arrays : arrays + 6]
    partial_ref, spread, outer_own, inverse_own = refs[arrays + 6 : arrays + 10]
    turned, inverse, outer = refs[arrays + 10 :]
    pairs = rows * total
    tiles = C * C // LANES
    per_tile = LANES // total
    me = lax.axis_index("pi")
    at_pairs = pairs + C + tiles * rows

    half = total // CORES
    row = iota((total, LANES), 0)
    core = lax.rem(me, CORES)
    step = jnp.zeros((total, LANES), jnp.int32)
    for m, offset in enumerate(offsets(route)):
        for k in range(CORES):
            at = row // rows == k * pieces + m
            step = jnp.where(at, jnp.where(core == k, offset[0], offset[1]) + k, step)
    source = lax.bitwise_xor(step, me) * rows + lax.rem(row, rows)
    place = (source == lax.rem(iota((total, LANES), 1), total)).astype(F32).astype(BF16)
    both = [
        jnp.concatenate([ref[t * half : (t + 1) * half, :] for ref in (own_ref, other_ref)], 0)
        for t in range(tiles + 1)
    ]
    for tile in range(tiles):
        turned[tile * LANES : (tile + 1) * LANES, :] = dot(both[tile], place, 0, 0)
    depth_lane = dot(both[tiles], place, 0, 0)

    for m in range(pieces):
        block = piece[m][at_pairs : at_pairs + 16, :].astype(F32)
        for tile in range(pairs // LANES):
            least = jnp.minimum(block[8 + tile : 9 + tile, :], depth_lane[:1, :])
            inverse[m : m + 1, tile * LANES : (tile + 1) * LANES] = 1.0 / (epsilon + least)

    alignment = spread.shape[0] // rows
    alive = iota((alignment, LANES), 0).astype(F32) < depth_lane[:alignment, :]
    part_of = iota((alignment, LANES), 1) // total
    keep = [jnp.where(alive & (part_of == k), 1.0, 0.0).astype(F32) for k in range(per_tile)]
    for d in range(C):
        block = turned[pl.ds(d, alignment, stride=C), :]
        kept = [(block * keep[k]).astype(BF16) for k in range(per_tile)]
        for i in range(rows):
            at = d * pairs + i // per_tile * LANES
            spread[i * alignment : (i + 1) * alignment, at : at + LANES] = kept[i % per_tile]

    chunk = 8
    for d in range(C):
        o = dot(left_all[...], spread[:, d * pairs : (d + 1) * pairs], 1, 0)
        for m in range(pieces):
            outer[d * C : (d + 1) * C, m * pairs : (m + 1) * pairs] = (
                o[m * C : (m + 1) * C, :] * inverse[m : m + 1, :]
            ).astype(BF16)
        if d % chunk == chunk - 1:
            first = d + 1 - chunk
            some = slice(first * C, (d + 1) * C)
            outer_own[some, :] = outer[some, :pairs]
            grad = dot(outer[some, :], cots[...], 1, 0)
            for k in range(chunk):
                partial_ref[pl.ds(first + k, C, stride=C), :] = grad[k * C : (k + 1) * C, :]
    wide = C * C
    last = wide + right_ref.shape[0]
    partial_ref[wide:last, :] = right_ref[...]
    partial_ref[last : last + 8, :] = dot(
        jnp.ones((8, pieces * pairs), BF16), cots[...], 1, 0
    )
    inverse_own[...] = inverse[...]


def own_kernel(
    rows, spread, outer_own, inverse_own, payload_ref, w_swap_ref, bias_ref,
    update_ref, left_ref, g_left, stage,
):
    some = 8
    pairs = update_ref.shape[0]
    alignment = spread.shape[0] // rows
    tiles = left_ref.shape[1] // LANES
    group = LANES // C
    update = dot(outer_own[...], w_swap_ref[...], 0, 0)
    update_ref[...] = (update + bias_ref[...]).astype(BF16)
    for d in range(C):
        if d % some == 0:
            g = dot(w_swap_ref[d * C : (d + some) * C, :], payload_ref[:pairs, :], 1, 1)
            g = (g * inverse_own[:1, :]).astype(BF16)
        g_left[:, d * pairs : (d + 1) * pairs] = g[d % some * C : (d % some + 1) * C, :]
    left_grad = dot(spread[...], g_left[...], 1, 1)
    stage[...] = jnp.concatenate([left_grad] * group, 1)
    in_tile = iota((8, LANES), 1) // C
    row_of = (iota((8, LANES), 0) * group + in_tile).astype(F32)
    at_depth = pairs + C + tiles * rows
    depth = payload_ref[at_depth : at_depth + 16, :].astype(F32)
    for i in range(rows):
        flat = jnp.zeros((8, LANES), F32)
        for q in range(group):
            flat = jnp.where(
                in_tile == q, stage[pl.ds(i * alignment + q, tiles, stride=group), :], flat
            )
        flat = jnp.where(row_of < depth[i : i + 1, :], flat, 0.0)
        for tile in range(tiles):
            left_ref[i : i + 1, tile * LANES : (tile + 1) * LANES] = flat[tile : tile + 1, :]


def swap(x, masks, size):
    return lax.ppermute(x, "pi", [(i, i ^ masks[i % CORES]) for i in range(size)])


def route_of(size):
    near, middle, far = CORES, size // 4, size // 2
    if near * 2 == middle:
        return (
            ((0,), (far,) * CORES),
            ((0,), (far + middle + near,) * CORES),
            ((1,), (middle,) * CORES),
            ((0,), (near,) * CORES),
            ((4,), (middle,) * CORES),
            ((0,), (middle,) * CORES),
            ((1,), (near,) * CORES),
        )
    return tuple(((0,), (offset,) * CORES) for offset in range(CORES, size, CORES))


def offsets(route):
    found = [(0,) * CORES]
    for sources, hops in route:
        found += [tuple(a ^ b for a, b in zip(found[k], hops)) for k in sources]
    return found


def gathered(left, right, depth, w_out, bias, pair_cot):
    rows, width = left.shape
    alignment = width // C
    total, channels = pair_cot.shape[1:]
    size = lax.axis_size("pi")
    pieces = size // CORES
    pairs = rows * total
    chip_rows = CORES * rows
    tiles = width // LANES
    used = pairs + C + tiles * rows + 16
    hbm = pl.BlockSpec(memory_space=pltpu.HBM)
    vmem = pl.BlockSpec(memory_space=pltpu.VMEM)
    depth_other = swap(depth, (1, 1), size)
    given = (
        left, right, pair_cot.reshape(pairs, channels), depth, bias.reshape(1, channels), w_out,
    )
    payload, bias_row, w_here = pl.pallas_call(
        pack_kernel,
        out_shape=(
            pltpu.VMEM((used, LANES), BF16),
            pltpu.VMEM((1, channels), F32),
            pltpu.VMEM(w_out.shape, BF16),
        ),
        in_specs=[hbm] * 6,
        out_specs=(vmem, vmem, vmem),
        scratch_shapes=[
            pltpu.VMEM(left.shape, BF16),
            pltpu.VMEM(right.shape, BF16),
            pltpu.SMEM(depth.shape, jnp.int32),
            pltpu.SemaphoreType.DMA((6,)),
        ],
        compiler_params=pltpu.CompilerParams(vmem_limit_bytes=SMALL),
        cost_estimate=pl.CostEstimate(flops=10**9, bytes_accessed=2**20, transcendentals=0),
    )(*[pltpu.with_memory_space_constraint(x, pltpu.HBM) for x in given])
    arrived = [payload]
    place = {0: payload}
    route = route_of(size)
    for sources, hops in route:
        message = [place[k] for k in sources]
        message = swap(jnp.concatenate(message, 0) if len(message) > 1 else message[0], hops, size)
        if len(sources) == 1:
            place[sum(x.shape[0] for x in arrived) // used] = message
        arrived.append(message)
    mine = pl.pallas_call(
        functools.partial(collect_kernel, used, pairs + C),
        out_shape=pltpu.VMEM((total // CORES * (tiles + 1), LANES), BF16),
        compiler_params=pltpu.CompilerParams(vmem_limit_bytes=SMALL),
    )(*arrived)
    theirs = swap(mine, (1, 1), size)
    count_lanes = chip_rows * rows * pieces
    w_swap, spread = pl.pallas_call(
        prepare_kernel,
        out_shape=(
            pltpu.VMEM(w_out.shape, BF16),
            pltpu.VMEM((rows * alignment, C * pairs), BF16),
        ),
        scratch_shapes=[pltpu.VMEM(w_out.shape, F32)],
        compiler_params=pltpu.CompilerParams(vmem_limit_bytes=SMALL),
    )(w_here, arrived[1])
    right_partial, cots, left_all = pl.pallas_call(
        functools.partial(right_kernel, (rows, total, pieces, alignment, used, len(arrived))),
        out_shape=(
            pltpu.VMEM((chip_rows * tiles, LANES), F32),
            pltpu.VMEM((pieces * pairs, channels), BF16),
            pltpu.VMEM((pieces * C, LANES), BF16),
        ),
        scratch_shapes=[
            pltpu.VMEM((pieces * C, LANES), F32),
            pltpu.VMEM((count_lanes, channels), F32),
            pltpu.VMEM((count_lanes, channels), BF16),
            pltpu.VMEM((C * LANES, LANES), BF16),
            pltpu.VMEM((count_lanes // LANES * C, C * LANES), BF16),
            pltpu.VMEM((LANES, LANES), F32),
            pltpu.VMEM((16, LANES), F32),
        ],
        compiler_params=pltpu.CompilerParams(vmem_limit_bytes=LARGE),
        cost_estimate=pl.CostEstimate(flops=10**9, bytes_accessed=2**20, transcendentals=0),
    )(*arrived, w_here, depth_other.reshape(1, rows))
    partial, spread, outer_own, inverse_own = pl.pallas_call(
        functools.partial(main_kernel, (rows, total, pieces, used, len(arrived), route)),
        out_shape=(
            pltpu.VMEM((C * C + chip_rows * tiles + 8, LANES), F32),
            pltpu.VMEM((rows * alignment, C * pairs), BF16),
            pltpu.VMEM((C * C, pairs), BF16),
            pltpu.VMEM((pieces, pairs), F32),
        ),
        scratch_shapes=[
            pltpu.VMEM((width, LANES), F32),
            pltpu.VMEM((pieces, pairs), F32),
            pltpu.VMEM((C * C, pieces * pairs), BF16),
        ],
        input_output_aliases={len(arrived) + 5: 1},
        compiler_params=pltpu.CompilerParams(vmem_limit_bytes=LARGE),
    )(*arrived, mine, theirs, right_partial, cots, left_all, spread)
    other = swap(partial, (1, 1), size)
    update, grad_left = pl.pallas_call(
        functools.partial(own_kernel, rows),
        out_shape=(pltpu.VMEM((pairs, channels), BF16), pltpu.VMEM((rows, width), F32)),
        scratch_shapes=[
            pltpu.VMEM((C, C * pairs), BF16),
            pltpu.VMEM((LANES, LANES), F32),
        ],
        compiler_params=pltpu.CompilerParams(vmem_limit_bytes=LARGE),
        cost_estimate=pl.CostEstimate(
            flops=8 * pairs * C * C * channels, bytes_accessed=4 * 2**20, transcendentals=0
        ),
    )(spread, outer_own, inverse_own, payload, w_swap, bias_row)
    update, grad_left, grad_w, grad_right, grad_bias = pl.pallas_call(
        functools.partial(sum_kernel, rows),
        out_shape=(
            jax.ShapeDtypeStruct((pairs, channels), BF16),
            jax.ShapeDtypeStruct((rows, width), F32),
            jax.ShapeDtypeStruct((C * C, channels), F32),
            jax.ShapeDtypeStruct((rows, width), F32),
            jax.ShapeDtypeStruct((1, channels), F32),
        ),
        out_specs=(hbm,) * 5,
        scratch_shapes=[
            pltpu.VMEM((C * C, channels), F32),
            pltpu.VMEM((rows, width), F32),
            pltpu.VMEM((1, channels), F32),
            pltpu.SemaphoreType.DMA((8,)),
        ],
        compiler_params=pltpu.CompilerParams(vmem_limit_bytes=SMALL),
    )(partial, other, update, grad_left)
    return (
        update.reshape(rows, total, channels),
        grad_left,
        grad_right,
        grad_w,
        grad_bias.reshape(channels),
    )


def gathers(left, pair_cot, w_out):
    rows, width = left.shape
    total, channels = pair_cot.shape[1:]
    size = lax.axis_size("pi")
    gather_bytes = size * pair_cot.size * 2
    reduce_bytes = 2 * w_out.size * 4
    return (
        gather_bytes <= reduce_bytes
        and size >= 2 * CORES
        and size & (size - 1) == 0
        and rows & (rows - 1) == 0
        and channels == LANES
        and rows * (width // C) == LANES
        and LANES % total == 0
        and width == C * C == 8 * LANES
        and rows * CORES == 8
        and (rows * size // CORES) * (LANES // C) == LANES
    )


def local(left, right, depth, w_out, bias, pair_cot):
    if gathers(left, pair_cot, w_out):
        return gathered(left, right, depth, w_out, bias, pair_cot)
    return reduced(left, right, depth, w_out, bias, pair_cot)


def reduced(left, right, depth, w_out, bias, pair_cot):
    rows = left.shape[0]
    width = left.shape[1]
    alignment = width // C
    total = pair_cot.shape[1]
    channels = w_out.shape[1]
    row_ids = jnp.arange(alignment, dtype=jnp.int32)
    own_mask = (row_ids[None, :] < depth[:, None]).astype(jnp.bfloat16)
    own_left = left.reshape(rows, alignment, C) * own_mask[:, :, None]
    w_back = w_out.T
    pair_cols = lax.all_to_all(pair_cot, "pi", split_axis=1, concat_axis=0, tiled=True)
    init = (
        jnp.zeros((rows, total, channels), jnp.bfloat16),
        jnp.zeros((rows, width), jnp.float32),
        jnp.zeros((C * C, channels), jnp.float32),
        jnp.zeros((channels,), jnp.float32),
    )
    carry = init
    start = jnp.int32(0)
    right_piece = lax.all_gather(right, "pi", axis=0, tiled=True)
    depth_piece = lax.all_gather(depth, "pi", axis=0, tiled=True)
    length = right_piece.shape[0]
    block = math.gcd(length, 256)
    for offset in range(0, length, block):
        begin = start + offset
        depth_block = depth_piece[offset : offset + block]
        mask_block = (row_ids[None, :] < depth_block[:, None]).astype(jnp.bfloat16)
        right_block = (
            right_piece[offset : offset + block].reshape(block, alignment, C)
            * mask_block[:, :, None]
        )
        count = epsilon + jnp.minimum(depth[:, None], depth_block[None, :]).astype(jnp.float32)
        outer = jnp.einsum(
            "isc,jsd->ijcd", own_left, right_block, preferred_element_type=jnp.float32
        )
        outer = (outer / count[:, :, None, None]).reshape(rows, block, C * C).astype(jnp.bfloat16)
        update = (jnp.dot(outer, w_out, preferred_element_type=jnp.float32) + bias).astype(
            jnp.bfloat16
        )
        cot_block = lax.dynamic_slice_in_dim(pair_cot, begin, block, 1)
        pair_out = lax.dynamic_update_slice(carry[0], update, (0, begin, 0))
        weight_acc = carry[2] + jnp.dot(
            outer.reshape(-1, C * C).T,
            cot_block.reshape(-1, channels),
            preferred_element_type=jnp.float32,
        )
        bias_acc = carry[3] + jnp.sum(cot_block, axis=(0, 1), dtype=jnp.float32)
        grad_pair = (
            jnp.dot(cot_block, w_back, preferred_element_type=jnp.float32) / count[:, :, None]
        )
        grad_pair = grad_pair.astype(jnp.bfloat16).reshape(rows, block, C, C)
        left_acc = carry[1] + jnp.einsum(
            "ijcd,jsd->isc", grad_pair, right_block, preferred_element_type=jnp.float32
        ).reshape(rows, width)
        carry = (pair_out, left_acc, weight_acc, bias_acc)
    pair_update = carry[0]
    left_acc = carry[1]
    accum = jnp.zeros((rows, width), jnp.float32)
    start = jnp.int32(0)
    left_piece = lax.all_gather(left, "pi", axis=0, tiled=True)
    depth_piece = lax.all_gather(depth, "pi", axis=0, tiled=True)
    length = left_piece.shape[0]
    block = math.gcd(length, 256)
    for offset in range(0, length, block):
        begin = start + offset
        depth_block = depth_piece[offset : offset + block]
        mask_block = (row_ids[None, :] < depth_block[:, None]).astype(jnp.bfloat16)
        left_block = (
            left_piece[offset : offset + block].reshape(block, alignment, C)
            * mask_block[:, :, None]
        )
        count = epsilon + jnp.minimum(depth_block[:, None], depth[None, :]).astype(jnp.float32)
        cot_block = lax.dynamic_slice_in_dim(pair_cols, begin, block, 0)
        grad_pair = (
            jnp.dot(cot_block, w_back, preferred_element_type=jnp.float32) / count[:, :, None]
        )
        grad_pair = grad_pair.astype(jnp.bfloat16).reshape(block, rows, C, C)
        accum = accum + jnp.einsum(
            "ijcd,isc->jsd", grad_pair, left_block, preferred_element_type=jnp.float32
        ).reshape(rows, width)
    grad_w, grad_bias = lax.psum((carry[2], carry[3]), "pi")
    grad_left = (left_acc.reshape(rows, alignment, C) * own_mask[:, :, None]).reshape(rows, width)
    grad_right = (accum.reshape(rows, alignment, C) * own_mask[:, :, None]).reshape(rows, width)
    return (pair_update, grad_left, grad_right, grad_w, grad_bias)


def solution(mesh):
    placed = (
        P(("grp", "pi"), None),
        P(("grp", "pi"), None),
        P(("grp", "pi")),
        P(),
        P(),
        P(("grp", "pi"), None, None),
    )
    return jax.shard_map(
        local,
        mesh=mesh,
        in_specs=placed,
        out_specs=(
            P(("grp", "pi"), None, None),
            P(("grp", "pi"), None),
            P(("grp", "pi"), None),
            P("grp", None),
            P("grp"),
        ),
        check_vma=False,
    )
```

```python
import functools
import math

import jax
import jax.numpy as jnp
from jax import lax
from jax.experimental import pallas as pl
from jax.experimental.pallas import tpu as pltpu
from jax.sharding import PartitionSpec as P

C = 32
LANES = 128
CORES = 2
SMALL = 8 * 2**20
LARGE = 24 * 2**20


epsilon = 0.001

F32 = jnp.float32
BF16 = jnp.bfloat16


def iota(shape, dim):
    return lax.broadcasted_iota(jnp.int32, shape, dim)


def dot(x, y, contract_x, contract_y):
    return lax.dot_general(
        x, y, (((contract_x,), (contract_y,)), ((), ())), preferred_element_type=F32
    )


def views(refs, used):
    return [
        ref.at[k * used : (k + 1) * used, :]
        for ref in refs
        for k in range(ref.shape[0] // used)
    ]


def pack_kernel(
    left_ref, right_ref, cot_ref, depth_ref, bias_ref, w_ref,
    payload_ref, bias_out_ref, w_out_ref,
    left_here, right_here, depth_here, sems,
):
    rows, width = left_here.shape
    pairs = cot_ref.shape[0]
    total = pairs // rows
    alignment = width // C
    tiles = width // LANES
    group = LANES // C
    chip_rows = CORES * rows
    ends = (
        (depth_ref, depth_here),
        (left_ref, left_here),
        (right_ref, right_here),
        (cot_ref, payload_ref.at[:pairs, :]),
        (bias_ref, bias_out_ref),
        (w_ref, w_out_ref),
    )
    copies = [pltpu.make_async_copy(*pair, sems.at[k]) for k, pair in enumerate(ends)]
    for copy in copies:
        copy.start()
    row = iota((tiles * rows, group * LANES), 0)
    lane = iota((tiles * rows, group * LANES), 1)
    target = lax.rem(row, rows) * alignment + row // rows * group + lane // LANES
    place = (lax.rem(lane, LANES) == target).astype(F32).astype(BF16)
    for copy in copies[:3]:
        copy.wait()
    left = left_here[...].astype(F32)
    flat = jnp.concatenate([left[:, t * LANES : (t + 1) * LANES] for t in range(tiles)], 0)
    flat = flat.astype(BF16)
    spots = dot(flat, place, 0, 0)
    turned = jnp.zeros((C, LANES), F32)
    for q in range(group):
        turned = turned + spots[q * C : (q + 1) * C, q * LANES : (q + 1) * LANES]
    lane = iota((C, LANES), 1)
    depth = jnp.zeros((C, LANES), jnp.int32)
    for i in range(rows):
        depth = jnp.where(lane // alignment == i, depth_here[i], depth)
    turned = jnp.where(lax.rem(lane, alignment) < depth, turned, 0.0)
    payload_ref[pairs : pairs + C, :] = turned.astype(BF16)
    own = right_here[...].astype(F32)
    parts = [own[:, t * LANES : (t + 1) * LANES] for t in range(tiles)]
    row = iota((8, LANES), 0)
    depth = jnp.zeros((8, LANES), jnp.int32)
    for i in range(rows):
        depth = jnp.where(row == i, depth_here[i], depth)
    parts.append(depth.astype(F32))
    lane = row * LANES + iota((8, LANES), 1)
    depth = jnp.zeros((8, LANES), jnp.int32)
    for i in range(rows):
        depth = jnp.where(lane // total == i, depth_here[i], depth)
    parts.append(depth.astype(F32))
    payload_ref[pairs + C :, :] = jnp.concatenate(parts, 0).astype(BF16)
    for copy in copies[3:]:
        copy.wait()


def collect_kernel(used, begin, *refs):
    piece, out_ref = views(refs[:-1], used), refs[-1]
    tail = [ref[begin:, :].astype(F32) for ref in piece]
    tiles = C * C // LANES + 1
    half = out_ref.shape[0] // tiles
    rows = half // len(piece)
    for tile in range(tiles):
        part = jnp.concatenate([x[tile * rows : (tile + 1) * rows] for x in tail], 0)
        out_ref[tile * half : (tile + 1) * half, :] = part.astype(BF16)


def sum_kernel(
    rows, own_ref, other_ref, update_here, left_here,
    update_ref, left_ref, w_ref, right_ref, bias_ref, w_here, right_here, bias_here, sems,
):
    copies = [
        pltpu.make_async_copy(update_here, update_ref, sems.at[0]),
        pltpu.make_async_copy(left_here, left_ref, sems.at[1]),
        pltpu.make_async_copy(right_here, right_ref, sems.at[2]),
        pltpu.make_async_copy(bias_here, bias_ref, sems.at[3]),
    ]
    copies[0].start()
    copies[1].start()
    wide = w_ref.shape[0]
    count = sems.shape[0] - 4
    for k in range(count):
        some = slice(k * wide // count, (k + 1) * wide // count)
        w_here[some, :] = own_ref[some, :] + other_ref[some, :]
        copies.append(pltpu.make_async_copy(w_here.at[some], w_ref.at[some], sems.at[4 + k]))
        copies[-1].start()
    core = lax.rem(lax.axis_index("pi"), CORES)
    tiles = right_ref.shape[1] // LANES
    begin = pl.multiple_of(wide + core * rows * tiles, 8)
    part = own_ref[pl.ds(begin, rows * tiles), :] + other_ref[pl.ds(begin, rows * tiles), :]
    for row in range(rows):
        for tile in range(tiles):
            at = row * tiles + tile
            right_here[row : row + 1, tile * LANES : (tile + 1) * LANES] = part[at : at + 1, :]
    last = wide + CORES * rows * tiles
    bias_here[...] = own_ref[last : last + 1, :] + other_ref[last : last + 1, :]
    copies[2].start()
    copies[3].start()
    for copy in copies:
        copy.wait()


def right_kernel(sizes, *refs):
    rows, total, pieces, alignment, used, arrays = sizes
    some = 8
    piece = views(refs[:arrays], used)
    w_ref, depth_ref, out_ref, cots, left_halves, w_swap_ref = refs[arrays : arrays + 6]
    left_wide, window, picked, weights, g_right, stage, depths, w_wide = refs[arrays + 6 :]
    chip_rows = CORES * rows
    pairs = rows * total
    tiles = C * C // LANES
    group = LANES // C
    me = lax.axis_index("pi")
    chip = me // CORES
    at_depth = pairs + C + tiles * rows

    for m in range(pieces):
        cots[m * pairs : (m + 1) * pairs, :] = piece[m][:pairs, :]
        left_wide[m * C : (m + 1) * C, :] = piece[m][pairs : pairs + C, :].astype(F32)
    width = left_halves.shape[1]
    for h in range(LANES // width):
        part = left_wide[...] if h == 0 else pltpu.roll(left_wide[...], LANES - h * width, 1)
        left_halves[h * pieces * C : (h + 1) * pieces * C, :] = part[:, :width].astype(BF16)
    w_wide[...] = w_ref[...].astype(F32)
    for d in range(C):
        w_swap_ref[d * C : (d + 1) * C, :] = w_wide[pl.ds(d, C, stride=C), :].astype(BF16)
    tail = [ref[at_depth : at_depth + 16, :].astype(F32)[:rows] for ref in piece]
    other = jnp.broadcast_to(depth_ref[...].astype(F32), (rows, rows))
    other = jnp.where(iota((rows, rows), 0) == iota((rows, rows), 1), other, 0.0)
    other = jnp.broadcast_to(jnp.sum(other, axis=1, keepdims=True), (rows, LANES))
    depths[...] = jnp.concatenate([tail[0], other, jnp.zeros((8, LANES), F32)], 0)
    half = lax.rem(chip, 16 // chip_rows)
    for m in range(pieces):
        for i in range(rows):
            begin = i * total + chip * chip_rows - half * chip_rows
            two = piece[m][pl.ds(pl.multiple_of(begin, 16), 16), :].astype(F32)
            one = two[:chip_rows]
            for k in range(1, 16 // chip_rows):
                one = jnp.where(half == k, two[k * chip_rows : (k + 1) * chip_rows], one)
            at = (i * pieces + m) * chip_rows
            window[at : at + chip_rows, :] = one
    mine = rows * pieces
    for j in range(chip_rows):
        picked[j * mine : (j + 1) * mine, :] = window[
            pl.ds(j, mine, stride=chip_rows), :
        ].astype(BF16)
    count_lanes = chip_rows * mine
    lane = lax.rem(iota((mine, count_lanes), 1), mine)
    from_i = iota((mine, count_lanes), 0) == lax.rem(lane, pieces) * rows + lane // pieces
    lane = iota((16, count_lanes), 1) // mine
    from_j = iota((16, count_lanes), 0) == lax.bitwise_xor(lane, lax.rem(me, CORES) * rows)
    depth_i = jnp.concatenate(tail, 0).astype(BF16)
    depth_i = dot(depth_i, from_i.astype(F32).astype(BF16), 0, 0)[:8, :]
    depth_j = dot(depths[...].astype(BF16), from_j.astype(F32).astype(BF16), 0, 0)[:8, :]
    inverse_right = (1.0 / (epsilon + jnp.minimum(depth_i, depth_j)))[:1, :]
    for c in range(C):
        if c % some == 0:
            g = dot(w_ref[c * C : (c + some) * C, :], picked[...], 1, 1)
            g = (g * inverse_right).astype(BF16)
        for k in range(count_lanes // LANES):
            g_right[k * C : (k + 1) * C, c * LANES : (c + 1) * LANES] = g[
                c % some * C : (c % some + 1) * C, k * LANES : (k + 1) * LANES
            ]
        feature = left_wide[pl.ds(c, pieces, stride=C), :]
        turns = [feature] + [pltpu.roll(feature, k * alignment, 1) for k in range(1, rows)]
        block_of = iota((pieces, LANES), 1) // alignment
        for j in range(group):
            both = jnp.concatenate(
                [jnp.where(block_of == j, turns[(j - i) % rows], 0.0) for i in range(rows)], 0
            )
            at = c * LANES + j * mine
            weights[at : at + mine, :] = both.astype(BF16)
    right_grad = dot(g_right[...], weights[...], 1, 0)
    in_tile = iota((8, LANES), 1) // C
    row_of = (iota((8, LANES), 0) * group + in_tile).astype(F32)
    for k in range(count_lanes // LANES):
        part = right_grad[k * C : (k + 1) * C, :]
        stage[...] = jnp.concatenate([part] * group, 0).T
        for j in range(group):
            flat = jnp.zeros((8, LANES), F32)
            for q in range(group):
                flat = jnp.where(
                    in_tile == q, stage[pl.ds(j * alignment + q, tiles, stride=group), :], flat
                )
            residue = lax.bitwise_xor(k * group + j, lax.rem(me, CORES) * rows)
            depth = depths[pl.ds(residue, 1), :]
            at = (k * group + j) * tiles
            out_ref[at : at + tiles, :] = jnp.where(row_of < depth, flat, 0.0)


def main_kernel(sizes, *refs):
    rows, total, pieces, used, arrays, route = sizes
    piece = views(refs[:arrays], used)
    own_ref, other_ref, right_ref, cots, left_halves = refs[arrays : arrays + 5]
    partial_ref, spread, outer_own, inverse_own = refs[arrays + 5 : arrays + 9]
    turned, inverse, outer = refs[arrays + 9 :]
    pairs = rows * total
    tiles = C * C // LANES
    per_tile = LANES // total
    me = lax.axis_index("pi")
    at_pairs = pairs + C + tiles * rows

    half = total // CORES
    row = iota((total, LANES), 0)
    core = lax.rem(me, CORES)
    step = jnp.zeros((total, LANES), jnp.int32)
    for m, offset in enumerate(offsets(route)):
        for k in range(CORES):
            at = row // rows == k * pieces + m
            step = jnp.where(at, jnp.where(core == k, offset[0], offset[1]) + k, step)
    source = lax.bitwise_xor(step, me) * rows + lax.rem(row, rows)
    place = (source == lax.rem(iota((total, LANES), 1), total)).astype(F32).astype(BF16)
    both = [
        jnp.concatenate([ref[t * half : (t + 1) * half, :] for ref in (own_ref, other_ref)], 0)
        for t in range(tiles + 1)
    ]
    for tile in range(tiles):
        turned[tile * LANES : (tile + 1) * LANES, :] = dot(both[tile], place, 0, 0)
    depth_lane = dot(both[tiles], place, 0, 0)

    for m in range(pieces):
        block = piece[m][at_pairs : at_pairs + 16, :].astype(F32)
        for tile in range(pairs // LANES):
            least = jnp.minimum(block[8 + tile : 9 + tile, :], depth_lane[:1, :])
            inverse[m : m + 1, tile * LANES : (tile + 1) * LANES] = 1.0 / (epsilon + least)

    alignment = spread.shape[0] // per_tile
    alive = iota((alignment, LANES), 0).astype(F32) < depth_lane[:alignment, :]
    part_of = iota((alignment, LANES), 1) // total
    keep = [jnp.where(alive & (part_of == k), 1.0, 0.0).astype(F32) for k in range(per_tile)]
    for d in range(C):
        block = turned[pl.ds(d, alignment, stride=C), :]
        for k in range(per_tile):
            spread[k * alignment : (k + 1) * alignment, d * LANES : (d + 1) * LANES] = (
                block * keep[k]
            ).astype(BF16)

    chunk = 8
    for d in range(C):
        if d % 2 == 0:
            two = spread[:, d * LANES : (d + 2) * LANES]
            parts = [
                dot(left_halves[h * pieces * C : (h + 1) * pieces * C, :], two, 1, 0)
                for h in range(pairs // LANES)
            ]
        for h in range(pairs // LANES):
            o = parts[h][:, d % 2 * LANES : (d % 2 + 1) * LANES]
            count = inverse[:, h * LANES : (h + 1) * LANES]
            for m in range(pieces):
                at = m * pairs + h * LANES
                outer[d * C : (d + 1) * C, at : at + LANES] = (
                    o[m * C : (m + 1) * C, :] * count[m : m + 1, :]
                ).astype(BF16)
        if d % chunk == chunk - 1:
            first = d + 1 - chunk
            some = slice(first * C, (d + 1) * C)
            outer_own[some, :] = outer[some, :pairs]
            grad = dot(outer[some, :], cots[...], 1, 0)
            for k in range(chunk):
                partial_ref[pl.ds(first + k, C, stride=C), :] = grad[k * C : (k + 1) * C, :]
    wide = C * C
    last = wide + right_ref.shape[0]
    partial_ref[wide:last, :] = right_ref[...]
    partial_ref[last : last + 8, :] = dot(
        jnp.ones((8, pieces * pairs), BF16), cots[...], 1, 0
    )
    inverse_own[...] = inverse[...]


def own_kernel(
    rows, spread, outer_own, inverse_own, payload_ref, w_swap_ref, bias_ref,
    update_ref, left_ref, g_left, stage,
):
    some = 8
    pairs = update_ref.shape[0]
    tiles = left_ref.shape[1] // LANES
    alignment = tiles * (LANES // C)
    halves = pairs // LANES
    group = LANES // C
    update = dot(outer_own[...], w_swap_ref[...], 0, 0)
    update_ref[...] = (update + bias_ref[...]).astype(BF16)
    for d in range(C):
        if d % some == 0:
            g = dot(w_swap_ref[d * C : (d + some) * C, :], payload_ref[:pairs, :], 1, 1)
            g = (g * inverse_own[:1, :]).astype(BF16)
        for h in range(halves):
            g_left[h * C : (h + 1) * C, d * LANES : (d + 1) * LANES] = g[
                d % some * C : (d % some + 1) * C, h * LANES : (h + 1) * LANES
            ]
    left_grad = dot(spread[...], g_left[...], 1, 1)
    for h in range(halves):
        part = left_grad[:, h * C : (h + 1) * C]
        stage[h * spread.shape[0] : (h + 1) * spread.shape[0], :] = jnp.concatenate(
            [part] * group, 1
        )
    in_tile = iota((8, LANES), 1) // C
    row_of = (iota((8, LANES), 0) * group + in_tile).astype(F32)
    at_depth = pairs + C + tiles * rows
    depth = payload_ref[at_depth : at_depth + 16, :].astype(F32)
    for i in range(rows):
        flat = jnp.zeros((8, LANES), F32)
        for q in range(group):
            flat = jnp.where(
                in_tile == q, stage[pl.ds(i * alignment + q, tiles, stride=group), :], flat
            )
        flat = jnp.where(row_of < depth[i : i + 1, :], flat, 0.0)
        for tile in range(tiles):
            left_ref[i : i + 1, tile * LANES : (tile + 1) * LANES] = flat[tile : tile + 1, :]


def swap(x, masks, size):
    return lax.ppermute(x, "pi", [(i, i ^ masks[i % CORES]) for i in range(size)])


def route_of(size):
    near, middle, far = CORES, size // 4, size // 2
    if near * 2 == middle:
        return (
            ((0,), (far,) * CORES),
            ((0,), (far + middle + near,) * CORES),
            ((1,), (middle,) * CORES),
            ((0,), (near,) * CORES),
            ((4,), (middle,) * CORES),
            ((0,), (middle,) * CORES),
            ((1,), (near,) * CORES),
        )
    return tuple(((0,), (offset,) * CORES) for offset in range(CORES, size, CORES))


def offsets(route):
    found = [(0,) * CORES]
    for sources, hops in route:
        found += [tuple(a ^ b for a, b in zip(found[k], hops)) for k in sources]
    return found


def gathered(left, right, depth, w_out, bias, pair_cot):
    rows, width = left.shape
    alignment = width // C
    total, channels = pair_cot.shape[1:]
    size = lax.axis_size("pi")
    pieces = size // CORES
    pairs = rows * total
    chip_rows = CORES * rows
    tiles = width // LANES
    used = pairs + C + tiles * rows + 16
    hbm = pl.BlockSpec(memory_space=pltpu.HBM)
    vmem = pl.BlockSpec(memory_space=pltpu.VMEM)
    depth_other = swap(depth, (1, 1), size)
    given = (
        left, right, pair_cot.reshape(pairs, channels), depth, bias.reshape(1, channels), w_out,
    )
    payload, bias_row, w_here = pl.pallas_call(
        pack_kernel,
        out_shape=(
            pltpu.VMEM((used, LANES), BF16),
            pltpu.VMEM((1, channels), F32),
            pltpu.VMEM(w_out.shape, BF16),
        ),
        in_specs=[hbm] * 6,
        out_specs=(vmem, vmem, vmem),
        scratch_shapes=[
            pltpu.VMEM(left.shape, BF16),
            pltpu.VMEM(right.shape, BF16),
            pltpu.SMEM(depth.shape, jnp.int32),
            pltpu.SemaphoreType.DMA((6,)),
        ],
        compiler_params=pltpu.CompilerParams(vmem_limit_bytes=SMALL),
        cost_estimate=pl.CostEstimate(flops=10**9, bytes_accessed=2**20, transcendentals=0),
    )(*[pltpu.with_memory_space_constraint(x, pltpu.HBM) for x in given])
    arrived = [payload]
    place = {0: payload}
    route = route_of(size)
    for sources, hops in route:
        message = [place[k] for k in sources]
        message = swap(jnp.concatenate(message, 0) if len(message) > 1 else message[0], hops, size)
        if len(sources) == 1:
            place[sum(x.shape[0] for x in arrived) // used] = message
        arrived.append(message)
    mine = pl.pallas_call(
        functools.partial(collect_kernel, used, pairs + C),
        out_shape=pltpu.VMEM((total // CORES * (tiles + 1), LANES), BF16),
        compiler_params=pltpu.CompilerParams(vmem_limit_bytes=SMALL),
    )(*arrived)
    theirs = swap(mine, (1, 1), size)
    count_lanes = chip_rows * rows * pieces
    per_tile = LANES // total
    right_partial, cots, left_halves, w_swap = pl.pallas_call(
        functools.partial(right_kernel, (rows, total, pieces, alignment, used, len(arrived))),
        out_shape=(
            pltpu.VMEM((chip_rows * tiles, LANES), F32),
            pltpu.VMEM((pieces * pairs, channels), BF16),
            pltpu.VMEM((rows // per_tile * pieces * C, per_tile * alignment), BF16),
            pltpu.VMEM(w_out.shape, BF16),
        ),
        scratch_shapes=[
            pltpu.VMEM((pieces * C, LANES), F32),
            pltpu.VMEM((count_lanes, channels), F32),
            pltpu.VMEM((count_lanes, channels), BF16),
            pltpu.VMEM((C * LANES, LANES), BF16),
            pltpu.VMEM((count_lanes // LANES * C, C * LANES), BF16),
            pltpu.VMEM((LANES, LANES), F32),
            pltpu.VMEM((16, LANES), F32),
            pltpu.VMEM(w_out.shape, F32),
        ],
        compiler_params=pltpu.CompilerParams(vmem_limit_bytes=LARGE),
        cost_estimate=pl.CostEstimate(flops=10**9, bytes_accessed=2**20, transcendentals=0),
    )(*arrived, w_here, depth_other.reshape(1, rows))
    partial, spread, outer_own, inverse_own = pl.pallas_call(
        functools.partial(main_kernel, (rows, total, pieces, used, len(arrived), route)),
        out_shape=(
            pltpu.VMEM((C * C + chip_rows * tiles + 8, LANES), F32),
            pltpu.VMEM((per_tile * alignment, C * LANES), BF16),
            pltpu.VMEM((C * C, pairs), BF16),
            pltpu.VMEM((pieces, pairs), F32),
        ),
        scratch_shapes=[
            pltpu.VMEM((width, LANES), F32),
            pltpu.VMEM((pieces, pairs), F32),
            pltpu.VMEM((C * C, pieces * pairs), BF16),
        ],
        compiler_params=pltpu.CompilerParams(vmem_limit_bytes=LARGE),
    )(*arrived, mine, theirs, right_partial, cots, left_halves)
    other = swap(partial, (1, 1), size)
    update, grad_left = pl.pallas_call(
        functools.partial(own_kernel, rows),
        out_shape=(pltpu.VMEM((pairs, channels), BF16), pltpu.VMEM((rows, width), F32)),
        scratch_shapes=[
            pltpu.VMEM((pairs // LANES * C, C * LANES), BF16),
            pltpu.VMEM((LANES, LANES), F32),
        ],
        compiler_params=pltpu.CompilerParams(vmem_limit_bytes=LARGE),
        cost_estimate=pl.CostEstimate(
            flops=8 * pairs * C * C * channels, bytes_accessed=4 * 2**20, transcendentals=0
        ),
    )(spread, outer_own, inverse_own, payload, w_swap, bias_row)
    update, grad_left, grad_w, grad_right, grad_bias = pl.pallas_call(
        functools.partial(sum_kernel, rows),
        out_shape=(
            jax.ShapeDtypeStruct((pairs, channels), BF16),
            jax.ShapeDtypeStruct((rows, width), F32),
            jax.ShapeDtypeStruct((C * C, channels), F32),
            jax.ShapeDtypeStruct((rows, width), F32),
            jax.ShapeDtypeStruct((1, channels), F32),
        ),
        out_specs=(hbm,) * 5,
        scratch_shapes=[
            pltpu.VMEM((C * C, channels), F32),
            pltpu.VMEM((rows, width), F32),
            pltpu.VMEM((1, channels), F32),
            pltpu.SemaphoreType.DMA((8,)),
        ],
        compiler_params=pltpu.CompilerParams(vmem_limit_bytes=SMALL),
    )(partial, other, update, grad_left)
    return (
        update.reshape(rows, total, channels),
        grad_left,
        grad_right,
        grad_w,
        grad_bias.reshape(channels),
    )


def gathers(left, pair_cot, w_out):
    rows, width = left.shape
    total, channels = pair_cot.shape[1:]
    size = lax.axis_size("pi")
    gather_bytes = size * pair_cot.size * 2
    reduce_bytes = 2 * w_out.size * 4
    return (
        gather_bytes <= reduce_bytes
        and size >= 2 * CORES
        and size & (size - 1) == 0
        and rows & (rows - 1) == 0
        and channels == LANES
        and rows * (width // C) == LANES
        and LANES % total == 0
        and width == C * C == 8 * LANES
        and rows * CORES == 8
        and (rows * size // CORES) * (LANES // C) == LANES
    )


def local(left, right, depth, w_out, bias, pair_cot):
    if gathers(left, pair_cot, w_out):
        return gathered(left, right, depth, w_out, bias, pair_cot)
    return reduced(left, right, depth, w_out, bias, pair_cot)


def reduced(left, right, depth, w_out, bias, pair_cot):
    rows = left.shape[0]
    width = left.shape[1]
    alignment = width // C
    total = pair_cot.shape[1]
    channels = w_out.shape[1]
    row_ids = jnp.arange(alignment, dtype=jnp.int32)
    own_mask = (row_ids[None, :] < depth[:, None]).astype(jnp.bfloat16)
    own_left = left.reshape(rows, alignment, C) * own_mask[:, :, None]
    w_back = w_out.T
    pair_cols = lax.all_to_all(pair_cot, "pi", split_axis=1, concat_axis=0, tiled=True)
    init = (
        jnp.zeros((rows, total, channels), jnp.bfloat16),
        jnp.zeros((rows, width), jnp.float32),
        jnp.zeros((C * C, channels), jnp.float32),
        jnp.zeros((channels,), jnp.float32),
    )
    carry = init
    start = jnp.int32(0)
    right_piece = lax.all_gather(right, "pi", axis=0, tiled=True)
    depth_piece = lax.all_gather(depth, "pi", axis=0, tiled=True)
    length = right_piece.shape[0]
    block = math.gcd(length, 256)
    for offset in range(0, length, block):
        begin = start + offset
        depth_block = depth_piece[offset : offset + block]
        mask_block = (row_ids[None, :] < depth_block[:, None]).astype(jnp.bfloat16)
        right_block = (
            right_piece[offset : offset + block].reshape(block, alignment, C)
            * mask_block[:, :, None]
        )
        count = epsilon + jnp.minimum(depth[:, None], depth_block[None, :]).astype(jnp.float32)
        outer = jnp.einsum(
            "isc,jsd->ijcd", own_left, right_block, preferred_element_type=jnp.float32
        )
        outer = (outer / count[:, :, None, None]).reshape(rows, block, C * C).astype(jnp.bfloat16)
        update = (jnp.dot(outer, w_out, preferred_element_type=jnp.float32) + bias).astype(
            jnp.bfloat16
        )
        cot_block = lax.dynamic_slice_in_dim(pair_cot, begin, block, 1)
        pair_out = lax.dynamic_update_slice(carry[0], update, (0, begin, 0))
        weight_acc = carry[2] + jnp.dot(
            outer.reshape(-1, C * C).T,
            cot_block.reshape(-1, channels),
            preferred_element_type=jnp.float32,
        )
        bias_acc = carry[3] + jnp.sum(cot_block, axis=(0, 1), dtype=jnp.float32)
        grad_pair = (
            jnp.dot(cot_block, w_back, preferred_element_type=jnp.float32) / count[:, :, None]
        )
        grad_pair = grad_pair.astype(jnp.bfloat16).reshape(rows, block, C, C)
        left_acc = carry[1] + jnp.einsum(
            "ijcd,jsd->isc", grad_pair, right_block, preferred_element_type=jnp.float32
        ).reshape(rows, width)
        carry = (pair_out, left_acc, weight_acc, bias_acc)
    pair_update = carry[0]
    left_acc = carry[1]
    accum = jnp.zeros((rows, width), jnp.float32)
    start = jnp.int32(0)
    left_piece = lax.all_gather(left, "pi", axis=0, tiled=True)
    depth_piece = lax.all_gather(depth, "pi", axis=0, tiled=True)
    length = left_piece.shape[0]
    block = math.gcd(length, 256)
    for offset in range(0, length, block):
        begin = start + offset
        depth_block = depth_piece[offset : offset + block]
        mask_block = (row_ids[None, :] < depth_block[:, None]).astype(jnp.bfloat16)
        left_block = (
            left_piece[offset : offset + block].reshape(block, alignment, C)
            * mask_block[:, :, None]
        )
        count = epsilon + jnp.minimum(depth_block[:, None], depth[None, :]).astype(jnp.float32)
        cot_block = lax.dynamic_slice_in_dim(pair_cols, begin, block, 0)
        grad_pair = (
            jnp.dot(cot_block, w_back, preferred_element_type=jnp.float32) / count[:, :, None]
        )
        grad_pair = grad_pair.astype(jnp.bfloat16).reshape(block, rows, C, C)
        accum = accum + jnp.einsum(
            "ijcd,isc->jsd", grad_pair, left_block, preferred_element_type=jnp.float32
        ).reshape(rows, width)
    grad_w, grad_bias = lax.psum((carry[2], carry[3]), "pi")
    grad_left = (left_acc.reshape(rows, alignment, C) * own_mask[:, :, None]).reshape(rows, width)
    grad_right = (accum.reshape(rows, alignment, C) * own_mask[:, :, None]).reshape(rows, width)
    return (pair_update, grad_left, grad_right, grad_w, grad_bias)


def solution(mesh):
    placed = (
        P(("grp", "pi"), None),
        P(("grp", "pi"), None),
        P(("grp", "pi")),
        P(),
        P(),
        P(("grp", "pi"), None, None),
    )
    return jax.shard_map(
        local,
        mesh=mesh,
        in_specs=placed,
        out_specs=(
            P(("grp", "pi"), None, None),
            P(("grp", "pi"), None),
            P(("grp", "pi"), None),
            P("grp", None),
            P("grp"),
        ),
        check_vma=False,
    )
```

```python
import functools
import math

import jax
import jax.numpy as jnp
from jax import lax
from jax.experimental import pallas as pl
from jax.experimental.pallas import tpu as pltpu
from jax.sharding import PartitionSpec as P

C = 32
LANES = 128
CORES = 2
SMALL = 8 * 2**20
LARGE = 24 * 2**20


epsilon = 0.001

F32 = jnp.float32
BF16 = jnp.bfloat16


def iota(shape, dim):
    return lax.broadcasted_iota(jnp.int32, shape, dim)


def dot(x, y, contract_x, contract_y):
    return lax.dot_general(
        x, y, (((contract_x,), (contract_y,)), ((), ())), preferred_element_type=F32
    )


def views(refs, used):
    return [
        ref.at[k * used : (k + 1) * used, :]
        for ref in refs
        for k in range(ref.shape[0] // used)
    ]


def pack_kernel(
    left_ref, right_ref, cot_ref, depth_ref, bias_ref, w_ref,
    payload_ref, bias_out_ref, w_out_ref,
    left_here, right_here, depth_here, sems,
):
    rows, width = left_here.shape
    pairs = cot_ref.shape[0]
    total = pairs // rows
    alignment = width // C
    tiles = width // LANES
    group = LANES // C
    chip_rows = CORES * rows
    ends = (
        (depth_ref, depth_here),
        (left_ref, left_here),
        (right_ref, right_here),
        (cot_ref, payload_ref.at[:pairs, :]),
        (bias_ref, bias_out_ref),
        (w_ref, w_out_ref),
    )
    copies = [pltpu.make_async_copy(*pair, sems.at[k]) for k, pair in enumerate(ends)]
    for copy in copies:
        copy.start()
    row = iota((tiles * rows, group * LANES), 0)
    lane = iota((tiles * rows, group * LANES), 1)
    target = lax.rem(row, rows) * alignment + row // rows * group + lane // LANES
    place = (lax.rem(lane, LANES) == target).astype(F32).astype(BF16)
    for copy in copies[:3]:
        copy.wait()
    left = left_here[...].astype(F32)
    flat = jnp.concatenate([left[:, t * LANES : (t + 1) * LANES] for t in range(tiles)], 0)
    flat = flat.astype(BF16)
    spots = dot(flat, place, 0, 0)
    turned = jnp.zeros((C, LANES), F32)
    for q in range(group):
        turned = turned + spots[q * C : (q + 1) * C, q * LANES : (q + 1) * LANES]
    lane = iota((C, LANES), 1)
    depth = jnp.zeros((C, LANES), jnp.int32)
    for i in range(rows):
        depth = jnp.where(lane // alignment == i, depth_here[i], depth)
    turned = jnp.where(lax.rem(lane, alignment) < depth, turned, 0.0)
    payload_ref[pairs : pairs + C, :] = turned.astype(BF16)
    own = right_here[...].astype(F32)
    parts = [own[:, t * LANES : (t + 1) * LANES] for t in range(tiles)]
    row = iota((8, LANES), 0)
    depth = jnp.zeros((8, LANES), jnp.int32)
    for i in range(rows):
        depth = jnp.where(row == i, depth_here[i], depth)
    parts.append(depth.astype(F32))
    lane = row * LANES + iota((8, LANES), 1)
    depth = jnp.zeros((8, LANES), jnp.int32)
    for i in range(rows):
        depth = jnp.where(lane // total == i, depth_here[i], depth)
    parts.append(depth.astype(F32))
    payload_ref[pairs + C :, :] = jnp.concatenate(parts, 0).astype(BF16)
    for copy in copies[3:]:
        copy.wait()


def collect_kernel(used, begin, *refs):
    piece, out_ref = views(refs[:-1], used), refs[-1]
    tail = [ref[begin:, :].astype(F32) for ref in piece]
    tiles = C * C // LANES + 1
    half = out_ref.shape[0] // tiles
    rows = half // len(piece)
    for tile in range(tiles):
        part = jnp.concatenate([x[tile * rows : (tile + 1) * rows] for x in tail], 0)
        out_ref[tile * half : (tile + 1) * half, :] = part.astype(BF16)


def sum_kernel(
    rows, upper_ref, upper_other_ref, own_ref, other_ref, update_here, left_here,
    update_ref, left_ref, w_ref, right_ref, bias_ref, w_here, right_here, bias_here, sems,
):
    copies = [
        pltpu.make_async_copy(update_here, update_ref, sems.at[0]),
        pltpu.make_async_copy(left_here, left_ref, sems.at[1]),
        pltpu.make_async_copy(right_here, right_ref, sems.at[2]),
        pltpu.make_async_copy(bias_here, bias_ref, sems.at[3]),
    ]
    copies[0].start()
    copies[1].start()
    wide = w_ref.shape[0]
    count = sems.shape[0] - 4
    for k in range(count):
        some = slice(k * wide // count, (k + 1) * wide // count)
        if k < count // 2:
            w_here[some, :] = upper_ref[some, :] + upper_other_ref[some, :]
        else:
            rest = slice(some.start - wide // 2, some.stop - wide // 2)
            w_here[some, :] = own_ref[rest, :] + other_ref[rest, :]
        copies.append(pltpu.make_async_copy(w_here.at[some], w_ref.at[some], sems.at[4 + k]))
        copies[-1].start()
    core = lax.rem(lax.axis_index("pi"), CORES)
    tiles = right_ref.shape[1] // LANES
    begin = pl.multiple_of(wide // 2 + core * rows * tiles, 8)
    part = own_ref[pl.ds(begin, rows * tiles), :] + other_ref[pl.ds(begin, rows * tiles), :]
    for row in range(rows):
        for tile in range(tiles):
            at = row * tiles + tile
            right_here[row : row + 1, tile * LANES : (tile + 1) * LANES] = part[at : at + 1, :]
    last = wide // 2 + CORES * rows * tiles
    bias_here[...] = own_ref[last : last + 1, :] + other_ref[last : last + 1, :]
    copies[2].start()
    copies[3].start()
    for copy in copies:
        copy.wait()


def right_kernel(sizes, *refs):
    rows, total, pieces, alignment, used, arrays = sizes
    some = 8
    piece = views(refs[:arrays], used)
    w_ref, depth_ref, out_ref, cots, left_halves, w_swap_ref = refs[arrays : arrays + 6]
    left_wide, window, picked, weights, g_right, stage, depths, w_wide = refs[arrays + 6 :]
    chip_rows = CORES * rows
    pairs = rows * total
    tiles = C * C // LANES
    group = LANES // C
    me = lax.axis_index("pi")
    chip = me // CORES
    at_depth = pairs + C + tiles * rows

    for m in range(pieces):
        cots[m * pairs : (m + 1) * pairs, :] = piece[m][:pairs, :]
        left_wide[m * C : (m + 1) * C, :] = piece[m][pairs : pairs + C, :].astype(F32)
    width = left_halves.shape[1]
    for h in range(LANES // width):
        part = left_wide[...] if h == 0 else pltpu.roll(left_wide[...], LANES - h * width, 1)
        left_halves[h * pieces * C : (h + 1) * pieces * C, :] = part[:, :width].astype(BF16)
    w_wide[...] = w_ref[...].astype(F32)
    for d in range(C):
        w_swap_ref[d * C : (d + 1) * C, :] = w_wide[pl.ds(d, C, stride=C), :].astype(BF16)
    tail = [ref[at_depth : at_depth + 16, :].astype(F32)[:rows] for ref in piece]
    other = jnp.broadcast_to(depth_ref[...].astype(F32), (rows, rows))
    other = jnp.where(iota((rows, rows), 0) == iota((rows, rows), 1), other, 0.0)
    other = jnp.broadcast_to(jnp.sum(other, axis=1, keepdims=True), (rows, LANES))
    depths[...] = jnp.concatenate([tail[0], other, jnp.zeros((8, LANES), F32)], 0)
    half = lax.rem(chip, 16 // chip_rows)
    for m in range(pieces):
        for i in range(rows):
            begin = i * total + chip * chip_rows - half * chip_rows
            two = piece[m][pl.ds(pl.multiple_of(begin, 16), 16), :].astype(F32)
            one = two[:chip_rows]
            for k in range(1, 16 // chip_rows):
                one = jnp.where(half == k, two[k * chip_rows : (k + 1) * chip_rows], one)
            at = (i * pieces + m) * chip_rows
            window[at : at + chip_rows, :] = one
    mine = rows * pieces
    for j in range(chip_rows):
        picked[j * mine : (j + 1) * mine, :] = window[
            pl.ds(j, mine, stride=chip_rows), :
        ].astype(BF16)
    count_lanes = chip_rows * mine
    lane = lax.rem(iota((mine, count_lanes), 1), mine)
    from_i = iota((mine, count_lanes), 0) == lax.rem(lane, pieces) * rows + lane // pieces
    lane = iota((16, count_lanes), 1) // mine
    from_j = iota((16, count_lanes), 0) == lax.bitwise_xor(lane, lax.rem(me, CORES) * rows)
    depth_i = jnp.concatenate(tail, 0).astype(BF16)
    depth_i = dot(depth_i, from_i.astype(F32).astype(BF16), 0, 0)[:8, :]
    depth_j = dot(depths[...].astype(BF16), from_j.astype(F32).astype(BF16), 0, 0)[:8, :]
    inverse_right = (1.0 / (epsilon + jnp.minimum(depth_i, depth_j)))[:1, :]
    for c in range(C):
        if c % some == 0:
            g = dot(w_ref[c * C : (c + some) * C, :], picked[...], 1, 1)
            g = (g * inverse_right).astype(BF16)
        for k in range(count_lanes // LANES):
            g_right[k * C : (k + 1) * C, c * LANES : (c + 1) * LANES] = g[
                c % some * C : (c % some + 1) * C, k * LANES : (k + 1) * LANES
            ]
        feature = left_wide[pl.ds(c, pieces, stride=C), :]
        turns = [feature] + [pltpu.roll(feature, k * alignment, 1) for k in range(1, rows)]
        block_of = iota((pieces, LANES), 1) // alignment
        for j in range(group):
            both = jnp.concatenate(
                [jnp.where(block_of == j, turns[(j - i) % rows], 0.0) for i in range(rows)], 0
            )
            at = c * LANES + j * mine
            weights[at : at + mine, :] = both.astype(BF16)
    right_grad = dot(g_right[...], weights[...], 1, 0)
    in_tile = iota((8, LANES), 1) // C
    row_of = (iota((8, LANES), 0) * group + in_tile).astype(F32)
    for k in range(count_lanes // LANES):
        part = right_grad[k * C : (k + 1) * C, :]
        stage[...] = jnp.concatenate([part] * group, 0).T
        for j in range(group):
            flat = jnp.zeros((8, LANES), F32)
            for q in range(group):
                flat = jnp.where(
                    in_tile == q, stage[pl.ds(j * alignment + q, tiles, stride=group), :], flat
                )
            residue = lax.bitwise_xor(k * group + j, lax.rem(me, CORES) * rows)
            depth = depths[pl.ds(residue, 1), :]
            at = (k * group + j) * tiles
            out_ref[at : at + tiles, :] = jnp.where(row_of < depth, flat, 0.0)


def main_kernel(sizes, *refs):
    rows, total, pieces, used, arrays, route = sizes
    piece = views(refs[:arrays], used)
    own_ref, other_ref, right_ref, cots, left_halves = refs[arrays : arrays + 5]
    upper_ref, partial_ref, spread, outer_own, inverse_own = refs[arrays + 5 : arrays + 10]
    turned, inverse, outer = refs[arrays + 10 :]
    pairs = rows * total
    tiles = C * C // LANES
    per_tile = LANES // total
    me = lax.axis_index("pi")
    at_pairs = pairs + C + tiles * rows

    half = total // CORES
    row = iota((total, LANES), 0)
    core = lax.rem(me, CORES)
    step = jnp.zeros((total, LANES), jnp.int32)
    for m, offset in enumerate(offsets(route)):
        for k in range(CORES):
            at = row // rows == k * pieces + m
            step = jnp.where(at, jnp.where(core == k, offset[0], offset[1]) + k, step)
    source = lax.bitwise_xor(step, me) * rows + lax.rem(row, rows)
    place = (source == lax.rem(iota((total, LANES), 1), total)).astype(F32).astype(BF16)
    both = [
        jnp.concatenate([ref[t * half : (t + 1) * half, :] for ref in (own_ref, other_ref)], 0)
        for t in range(tiles + 1)
    ]
    for tile in range(tiles):
        turned[tile * LANES : (tile + 1) * LANES, :] = dot(both[tile], place, 0, 0)
    depth_lane = dot(both[tiles], place, 0, 0)

    for m in range(pieces):
        block = piece[m][at_pairs : at_pairs + 16, :].astype(F32)
        for tile in range(pairs // LANES):
            least = jnp.minimum(block[8 + tile : 9 + tile, :], depth_lane[:1, :])
            inverse[m : m + 1, tile * LANES : (tile + 1) * LANES] = 1.0 / (epsilon + least)

    alignment = spread.shape[0] // per_tile
    alive = iota((alignment, LANES), 0).astype(F32) < depth_lane[:alignment, :]
    part_of = iota((alignment, LANES), 1) // total
    keep = [jnp.where(alive & (part_of == k), 1.0, 0.0).astype(F32) for k in range(per_tile)]
    for d in range(C):
        block = turned[pl.ds(d, alignment, stride=C), :]
        for k in range(per_tile):
            spread[k * alignment : (k + 1) * alignment, d * LANES : (d + 1) * LANES] = (
                block * keep[k]
            ).astype(BF16)

    chunk = 8
    for d in range(C):
        if d % 2 == 0:
            two = spread[:, d * LANES : (d + 2) * LANES]
            parts = [
                dot(left_halves[h * pieces * C : (h + 1) * pieces * C, :], two, 1, 0)
                for h in range(pairs // LANES)
            ]
        for h in range(pairs // LANES):
            o = parts[h][:, d % 2 * LANES : (d % 2 + 1) * LANES]
            count = inverse[:, h * LANES : (h + 1) * LANES]
            for m in range(pieces):
                at = m * pairs + h * LANES
                outer[d * C : (d + 1) * C, at : at + LANES] = (
                    o[m * C : (m + 1) * C, :] * count[m : m + 1, :]
                ).astype(BF16)
        if d % chunk == chunk - 1:
            first = d + 1 - chunk
            some = slice(first * C, (d + 1) * C)
            outer_own[some, :] = outer[some, :pairs]
            grad = dot(outer[some, :], cots[...], 1, 0)
            for k in range(chunk):
                half = C // 2
                begin = k * C
                upper_ref[pl.ds(first + k, half, stride=C), :] = grad[begin : begin + half, :]
                partial_ref[pl.ds(first + k, half, stride=C), :] = grad[
                    begin + half : begin + C, :
                ]
    wide = C * C // 2
    last = wide + right_ref.shape[0]
    partial_ref[wide:last, :] = right_ref[...]
    partial_ref[last : last + 8, :] = dot(
        jnp.ones((8, pieces * pairs), BF16), cots[...], 1, 0
    )
    inverse_own[...] = inverse[...]


def own_kernel(
    rows, spread, outer_own, inverse_own, payload_ref, w_swap_ref, bias_ref,
    update_ref, left_ref, g_left, stage,
):
    some = 8
    pairs = update_ref.shape[0]
    tiles = left_ref.shape[1] // LANES
    alignment = tiles * (LANES // C)
    halves = pairs // LANES
    group = LANES // C
    update = dot(outer_own[...], w_swap_ref[...], 0, 0)
    update_ref[...] = (update + bias_ref[...]).astype(BF16)
    for d in range(C):
        if d % some == 0:
            g = dot(w_swap_ref[d * C : (d + some) * C, :], payload_ref[:pairs, :], 1, 1)
            g = (g * inverse_own[:1, :]).astype(BF16)
        for h in range(halves):
            g_left[h * C : (h + 1) * C, d * LANES : (d + 1) * LANES] = g[
                d % some * C : (d % some + 1) * C, h * LANES : (h + 1) * LANES
            ]
    left_grad = dot(spread[...], g_left[...], 1, 1)
    for h in range(halves):
        part = left_grad[:, h * C : (h + 1) * C]
        stage[h * spread.shape[0] : (h + 1) * spread.shape[0], :] = jnp.concatenate(
            [part] * group, 1
        )
    in_tile = iota((8, LANES), 1) // C
    row_of = (iota((8, LANES), 0) * group + in_tile).astype(F32)
    at_depth = pairs + C + tiles * rows
    depth = payload_ref[at_depth : at_depth + 16, :].astype(F32)
    for i in range(rows):
        flat = jnp.zeros((8, LANES), F32)
        for q in range(group):
            flat = jnp.where(
                in_tile == q, stage[pl.ds(i * alignment + q, tiles, stride=group), :], flat
            )
        flat = jnp.where(row_of < depth[i : i + 1, :], flat, 0.0)
        for tile in range(tiles):
            left_ref[i : i + 1, tile * LANES : (tile + 1) * LANES] = flat[tile : tile + 1, :]


def swap(x, masks, size):
    return lax.ppermute(x, "pi", [(i, i ^ masks[i % CORES]) for i in range(size)])


def route_of(size):
    near, middle, far = CORES, size // 4, size // 2
    if near * 2 == middle:
        return (
            ((0,), (far,) * CORES),
            ((0,), (far + middle + near,) * CORES),
            ((1,), (middle,) * CORES),
            ((0,), (near,) * CORES),
            ((4,), (middle,) * CORES),
            ((0,), (middle,) * CORES),
            ((1,), (near,) * CORES),
        )
    return tuple(((0,), (offset,) * CORES) for offset in range(CORES, size, CORES))


def offsets(route):
    found = [(0,) * CORES]
    for sources, hops in route:
        found += [tuple(a ^ b for a, b in zip(found[k], hops)) for k in sources]
    return found


def gathered(left, right, depth, w_out, bias, pair_cot):
    rows, width = left.shape
    alignment = width // C
    total, channels = pair_cot.shape[1:]
    size = lax.axis_size("pi")
    pieces = size // CORES
    pairs = rows * total
    chip_rows = CORES * rows
    tiles = width // LANES
    used = pairs + C + tiles * rows + 16
    hbm = pl.BlockSpec(memory_space=pltpu.HBM)
    vmem = pl.BlockSpec(memory_space=pltpu.VMEM)
    depth_other = swap(depth, (1, 1), size)
    given = (
        left, right, pair_cot.reshape(pairs, channels), depth, bias.reshape(1, channels), w_out,
    )
    payload, bias_row, w_here = pl.pallas_call(
        pack_kernel,
        out_shape=(
            pltpu.VMEM((used, LANES), BF16),
            pltpu.VMEM((1, channels), F32),
            pltpu.VMEM(w_out.shape, BF16),
        ),
        in_specs=[hbm] * 6,
        out_specs=(vmem, vmem, vmem),
        scratch_shapes=[
            pltpu.VMEM(left.shape, BF16),
            pltpu.VMEM(right.shape, BF16),
            pltpu.SMEM(depth.shape, jnp.int32),
            pltpu.SemaphoreType.DMA((6,)),
        ],
        compiler_params=pltpu.CompilerParams(vmem_limit_bytes=SMALL),
        cost_estimate=pl.CostEstimate(flops=10**9, bytes_accessed=2**20, transcendentals=0),
    )(*[pltpu.with_memory_space_constraint(x, pltpu.HBM) for x in given])
    arrived = [payload]
    place = {0: payload}
    route = route_of(size)
    for sources, hops in route:
        message = [place[k] for k in sources]
        message = swap(jnp.concatenate(message, 0) if len(message) > 1 else message[0], hops, size)
        if len(sources) == 1:
            place[sum(x.shape[0] for x in arrived) // used] = message
        arrived.append(message)
    mine = pl.pallas_call(
        functools.partial(collect_kernel, used, pairs + C),
        out_shape=pltpu.VMEM((total // CORES * (tiles + 1), LANES), BF16),
        compiler_params=pltpu.CompilerParams(vmem_limit_bytes=SMALL),
    )(*arrived)
    theirs = swap(mine, (1, 1), size)
    count_lanes = chip_rows * rows * pieces
    per_tile = LANES // total
    right_partial, cots, left_halves, w_swap = pl.pallas_call(
        functools.partial(right_kernel, (rows, total, pieces, alignment, used, len(arrived))),
        out_shape=(
            pltpu.VMEM((chip_rows * tiles, LANES), F32),
            pltpu.VMEM((pieces * pairs, channels), BF16),
            pltpu.VMEM((rows // per_tile * pieces * C, per_tile * alignment), BF16),
            pltpu.VMEM(w_out.shape, BF16),
        ),
        scratch_shapes=[
            pltpu.VMEM((pieces * C, LANES), F32),
            pltpu.VMEM((count_lanes, channels), F32),
            pltpu.VMEM((count_lanes, channels), BF16),
            pltpu.VMEM((C * LANES, LANES), BF16),
            pltpu.VMEM((count_lanes // LANES * C, C * LANES), BF16),
            pltpu.VMEM((LANES, LANES), F32),
            pltpu.VMEM((16, LANES), F32),
            pltpu.VMEM(w_out.shape, F32),
        ],
        compiler_params=pltpu.CompilerParams(vmem_limit_bytes=LARGE),
        cost_estimate=pl.CostEstimate(flops=10**9, bytes_accessed=2**20, transcendentals=0),
    )(*arrived, w_here, depth_other.reshape(1, rows))
    upper, partial, spread, outer_own, inverse_own = pl.pallas_call(
        functools.partial(main_kernel, (rows, total, pieces, used, len(arrived), route)),
        out_shape=(
            pltpu.VMEM((C * C // 2, LANES), F32),
            pltpu.VMEM((C * C // 2 + chip_rows * tiles + 8, LANES), F32),
            pltpu.VMEM((per_tile * alignment, C * LANES), BF16),
            pltpu.VMEM((C * C, pairs), BF16),
            pltpu.VMEM((pieces, pairs), F32),
        ),
        scratch_shapes=[
            pltpu.VMEM((width, LANES), F32),
            pltpu.VMEM((pieces, pairs), F32),
            pltpu.VMEM((C * C, pieces * pairs), BF16),
        ],
        compiler_params=pltpu.CompilerParams(vmem_limit_bytes=LARGE),
    )(*arrived, mine, theirs, right_partial, cots, left_halves)
    upper_other = swap(upper, (1, 1), size)
    other = swap(partial, (1, 1), size)
    update, grad_left = pl.pallas_call(
        functools.partial(own_kernel, rows),
        out_shape=(pltpu.VMEM((pairs, channels), BF16), pltpu.VMEM((rows, width), F32)),
        scratch_shapes=[
            pltpu.VMEM((pairs // LANES * C, C * LANES), BF16),
            pltpu.VMEM((LANES, LANES), F32),
        ],
        compiler_params=pltpu.CompilerParams(vmem_limit_bytes=LARGE),
        cost_estimate=pl.CostEstimate(
            flops=8 * pairs * C * C * channels, bytes_accessed=4 * 2**20, transcendentals=0
        ),
    )(spread, outer_own, inverse_own, payload, w_swap, bias_row)
    update, grad_left, grad_w, grad_right, grad_bias = pl.pallas_call(
        functools.partial(sum_kernel, rows),
        out_shape=(
            jax.ShapeDtypeStruct((pairs, channels), BF16),
            jax.ShapeDtypeStruct((rows, width), F32),
            jax.ShapeDtypeStruct((C * C, channels), F32),
            jax.ShapeDtypeStruct((rows, width), F32),
            jax.ShapeDtypeStruct((1, channels), F32),
        ),
        out_specs=(hbm,) * 5,
        scratch_shapes=[
            pltpu.VMEM((C * C, channels), F32),
            pltpu.VMEM((rows, width), F32),
            pltpu.VMEM((1, channels), F32),
            pltpu.SemaphoreType.DMA((8,)),
        ],
        compiler_params=pltpu.CompilerParams(vmem_limit_bytes=SMALL),
    )(upper, upper_other, partial, other, update, grad_left)
    return (
        update.reshape(rows, total, channels),
        grad_left,
        grad_right,
        grad_w,
        grad_bias.reshape(channels),
    )


def gathers(left, pair_cot, w_out):
    rows, width = left.shape
    total, channels = pair_cot.shape[1:]
    size = lax.axis_size("pi")
    gather_bytes = size * pair_cot.size * 2
    reduce_bytes = 2 * w_out.size * 4
    return (
        gather_bytes <= reduce_bytes
        and size >= 2 * CORES
        and size & (size - 1) == 0
        and rows & (rows - 1) == 0
        and channels == LANES
        and rows * (width // C) == LANES
        and LANES % total == 0
        and width == C * C == 8 * LANES
        and rows * CORES == 8
        and (rows * size // CORES) * (LANES // C) == LANES
    )


def local(left, right, depth, w_out, bias, pair_cot):
    if gathers(left, pair_cot, w_out):
        return gathered(left, right, depth, w_out, bias, pair_cot)
    return reduced(left, right, depth, w_out, bias, pair_cot)


def reduced(left, right, depth, w_out, bias, pair_cot):
    rows = left.shape[0]
    width = left.shape[1]
    alignment = width // C
    total = pair_cot.shape[1]
    channels = w_out.shape[1]
    row_ids = jnp.arange(alignment, dtype=jnp.int32)
    own_mask = (row_ids[None, :] < depth[:, None]).astype(jnp.bfloat16)
    own_left = left.reshape(rows, alignment, C) * own_mask[:, :, None]
    w_back = w_out.T
    pair_cols = lax.all_to_all(pair_cot, "pi", split_axis=1, concat_axis=0, tiled=True)
    init = (
        jnp.zeros((rows, total, channels), jnp.bfloat16),
        jnp.zeros((rows, width), jnp.float32),
        jnp.zeros((C * C, channels), jnp.float32),
        jnp.zeros((channels,), jnp.float32),
    )
    carry = init
    start = jnp.int32(0)
    right_piece = lax.all_gather(right, "pi", axis=0, tiled=True)
    depth_piece = lax.all_gather(depth, "pi", axis=0, tiled=True)
    length = right_piece.shape[0]
    block = math.gcd(length, 256)
    for offset in range(0, length, block):
        begin = start + offset
        depth_block = depth_piece[offset : offset + block]
        mask_block = (row_ids[None, :] < depth_block[:, None]).astype(jnp.bfloat16)
        right_block = (
            right_piece[offset : offset + block].reshape(block, alignment, C)
            * mask_block[:, :, None]
        )
        count = epsilon + jnp.minimum(depth[:, None], depth_block[None, :]).astype(jnp.float32)
        outer = jnp.einsum(
            "isc,jsd->ijcd", own_left, right_block, preferred_element_type=jnp.float32
        )
        outer = (outer / count[:, :, None, None]).reshape(rows, block, C * C).astype(jnp.bfloat16)
        update = (jnp.dot(outer, w_out, preferred_element_type=jnp.float32) + bias).astype(
            jnp.bfloat16
        )
        cot_block = lax.dynamic_slice_in_dim(pair_cot, begin, block, 1)
        pair_out = lax.dynamic_update_slice(carry[0], update, (0, begin, 0))
        weight_acc = carry[2] + jnp.dot(
            outer.reshape(-1, C * C).T,
            cot_block.reshape(-1, channels),
            preferred_element_type=jnp.float32,
        )
        bias_acc = carry[3] + jnp.sum(cot_block, axis=(0, 1), dtype=jnp.float32)
        grad_pair = (
            jnp.dot(cot_block, w_back, preferred_element_type=jnp.float32) / count[:, :, None]
        )
        grad_pair = grad_pair.astype(jnp.bfloat16).reshape(rows, block, C, C)
        left_acc = carry[1] + jnp.einsum(
            "ijcd,jsd->isc", grad_pair, right_block, preferred_element_type=jnp.float32
        ).reshape(rows, width)
        carry = (pair_out, left_acc, weight_acc, bias_acc)
    pair_update = carry[0]
    left_acc = carry[1]
    accum = jnp.zeros((rows, width), jnp.float32)
    start = jnp.int32(0)
    left_piece = lax.all_gather(left, "pi", axis=0, tiled=True)
    depth_piece = lax.all_gather(depth, "pi", axis=0, tiled=True)
    length = left_piece.shape[0]
    block = math.gcd(length, 256)
    for offset in range(0, length, block):
        begin = start + offset
        depth_block = depth_piece[offset : offset + block]
        mask_block = (row_ids[None, :] < depth_block[:, None]).astype(jnp.bfloat16)
        left_block = (
            left_piece[offset : offset + block].reshape(block, alignment, C)
            * mask_block[:, :, None]
        )
        count = epsilon + jnp.minimum(depth_block[:, None], depth[None, :]).astype(jnp.float32)
        cot_block = lax.dynamic_slice_in_dim(pair_cols, begin, block, 0)
        grad_pair = (
            jnp.dot(cot_block, w_back, preferred_element_type=jnp.float32) / count[:, :, None]
        )
        grad_pair = grad_pair.astype(jnp.bfloat16).reshape(block, rows, C, C)
        accum = accum + jnp.einsum(
            "ijcd,isc->jsd", grad_pair, left_block, preferred_element_type=jnp.float32
        ).reshape(rows, width)
    grad_w, grad_bias = lax.psum((carry[2], carry[3]), "pi")
    grad_left = (left_acc.reshape(rows, alignment, C) * own_mask[:, :, None]).reshape(rows, width)
    grad_right = (accum.reshape(rows, alignment, C) * own_mask[:, :, None]).reshape(rows, width)
    return (pair_update, grad_left, grad_right, grad_w, grad_bias)


def solution(mesh):
    placed = (
        P(("grp", "pi"), None),
        P(("grp", "pi"), None),
        P(("grp", "pi")),
        P(),
        P(),
        P(("grp", "pi"), None, None),
    )
    return jax.shard_map(
        local,
        mesh=mesh,
        in_specs=placed,
        out_specs=(
            P(("grp", "pi"), None, None),
            P(("grp", "pi"), None),
            P(("grp", "pi"), None),
            P("grp", None),
            P("grp"),
        ),
        check_vma=False,
    )
```

```python
import functools
import math

import jax
import jax.numpy as jnp
from jax import lax
from jax.experimental import pallas as pl
from jax.experimental.pallas import tpu as pltpu
from jax.sharding import PartitionSpec as P

C = 32
LANES = 128
CORES = 2
SMALL = 8 * 2**20
LARGE = 24 * 2**20


epsilon = 0.001

F32 = jnp.float32
BF16 = jnp.bfloat16


def iota(shape, dim):
    return lax.broadcasted_iota(jnp.int32, shape, dim)


def dot(x, y, contract_x, contract_y):
    return lax.dot_general(
        x, y, (((contract_x,), (contract_y,)), ((), ())), preferred_element_type=F32
    )


def views(refs, used):
    return [
        ref.at[k * used : (k + 1) * used, :]
        for ref in refs
        for k in range(ref.shape[0] // used)
    ]


def pack_kernel(
    left_ref, right_ref, cot_ref, depth_ref, bias_ref, w_ref,
    payload_ref, bias_out_ref, w_out_ref,
    left_here, right_here, depth_here, sems,
):
    rows, width = left_here.shape
    pairs = cot_ref.shape[0]
    total = pairs // rows
    alignment = width // C
    tiles = width // LANES
    group = LANES // C
    chip_rows = CORES * rows
    ends = (
        (depth_ref, depth_here),
        (left_ref, left_here),
        (right_ref, right_here),
        (cot_ref, payload_ref.at[:pairs, :]),
        (bias_ref, bias_out_ref),
        (w_ref, w_out_ref),
    )
    copies = [pltpu.make_async_copy(*pair, sems.at[k]) for k, pair in enumerate(ends)]
    for copy in copies:
        copy.start()
    row = iota((tiles * rows, group * LANES), 0)
    lane = iota((tiles * rows, group * LANES), 1)
    target = lax.rem(row, rows) * alignment + row // rows * group + lane // LANES
    place = (lax.rem(lane, LANES) == target).astype(F32).astype(BF16)
    for copy in copies[:3]:
        copy.wait()
    left = left_here[...].astype(F32)
    flat = jnp.concatenate([left[:, t * LANES : (t + 1) * LANES] for t in range(tiles)], 0)
    flat = flat.astype(BF16)
    spots = dot(flat, place, 0, 0)
    turned = jnp.zeros((C, LANES), F32)
    for q in range(group):
        turned = turned + spots[q * C : (q + 1) * C, q * LANES : (q + 1) * LANES]
    lane = iota((C, LANES), 1)
    depth = jnp.zeros((C, LANES), jnp.int32)
    for i in range(rows):
        depth = jnp.where(lane // alignment == i, depth_here[i], depth)
    turned = jnp.where(lax.rem(lane, alignment) < depth, turned, 0.0)
    payload_ref[pairs : pairs + C, :] = turned.astype(BF16)
    own = right_here[...].astype(F32)
    parts = [own[:, t * LANES : (t + 1) * LANES] for t in range(tiles)]
    row = iota((8, LANES), 0)
    depth = jnp.zeros((8, LANES), jnp.int32)
    for i in range(rows):
        depth = jnp.where(row == i, depth_here[i], depth)
    parts.append(depth.astype(F32))
    lane = row * LANES + iota((8, LANES), 1)
    depth = jnp.zeros((8, LANES), jnp.int32)
    for i in range(rows):
        depth = jnp.where(lane // total == i, depth_here[i], depth)
    parts.append(depth.astype(F32))
    payload_ref[pairs + C :, :] = jnp.concatenate(parts, 0).astype(BF16)
    for copy in copies[3:]:
        copy.wait()


def collect_kernel(used, begin, *refs):
    piece, out_ref = views(refs[:-1], used), refs[-1]
    tail = [ref[begin:, :].astype(F32) for ref in piece]
    tiles = C * C // LANES + 1
    half = out_ref.shape[0] // tiles
    rows = half // len(piece)
    for tile in range(tiles):
        part = jnp.concatenate([x[tile * rows : (tile + 1) * rows] for x in tail], 0)
        out_ref[tile * half : (tile + 1) * half, :] = part.astype(BF16)


def sum_kernel(
    rows, own_ref, other_ref, update_here, left_here,
    update_ref, left_ref, w_ref, right_ref, bias_ref, w_here, right_here, bias_here, sems,
):
    copies = [
        pltpu.make_async_copy(update_here, update_ref, sems.at[0]),
        pltpu.make_async_copy(left_here, left_ref, sems.at[1]),
        pltpu.make_async_copy(right_here, right_ref, sems.at[2]),
        pltpu.make_async_copy(bias_here, bias_ref, sems.at[3]),
    ]
    copies[0].start()
    copies[1].start()
    wide = w_ref.shape[0]
    count = sems.shape[0] - 4
    for k in range(count):
        some = slice(k * wide // count, (k + 1) * wide // count)
        w_here[some, :] = own_ref[some, :] + other_ref[some, :]
        copies.append(pltpu.make_async_copy(w_here.at[some], w_ref.at[some], sems.at[4 + k]))
        copies[-1].start()
    core = lax.rem(lax.axis_index("pi"), CORES)
    tiles = right_ref.shape[1] // LANES
    begin = pl.multiple_of(wide + core * rows * tiles, 8)
    part = own_ref[pl.ds(begin, rows * tiles), :] + other_ref[pl.ds(begin, rows * tiles), :]
    for row in range(rows):
        for tile in range(tiles):
            at = row * tiles + tile
            right_here[row : row + 1, tile * LANES : (tile + 1) * LANES] = part[at : at + 1, :]
    last = wide + CORES * rows * tiles
    bias_here[...] = own_ref[last : last + 1, :] + other_ref[last : last + 1, :]
    copies[2].start()
    copies[3].start()
    for copy in copies:
        copy.wait()


def right_kernel(sizes, *refs):
    rows, total, pieces, alignment, used, arrays = sizes
    some = 8
    piece = views(refs[:arrays], used)
    w_ref, depth_ref, out_ref, cots, left_halves, w_swap_ref = refs[arrays : arrays + 6]
    left_wide, window, picked, weights, g_right, stage, depths, w_wide = refs[arrays + 6 :]
    chip_rows = CORES * rows
    pairs = rows * total
    tiles = C * C // LANES
    group = LANES // C
    me = lax.axis_index("pi")
    chip = me // CORES
    at_depth = pairs + C + tiles * rows

    for m in range(pieces):
        cots[m * pairs : (m + 1) * pairs, :] = piece[m][:pairs, :]
        left_wide[m * C : (m + 1) * C, :] = piece[m][pairs : pairs + C, :].astype(F32)
    width = left_halves.shape[1]
    for h in range(LANES // width):
        part = left_wide[...] if h == 0 else pltpu.roll(left_wide[...], LANES - h * width, 1)
        left_halves[h * pieces * C : (h + 1) * pieces * C, :] = part[:, :width].astype(BF16)
    w_wide[...] = w_ref[...].astype(F32)
    for d in range(C):
        w_swap_ref[d * C : (d + 1) * C, :] = w_wide[pl.ds(d, C, stride=C), :].astype(BF16)
    tail = [ref[at_depth : at_depth + 16, :].astype(F32)[:rows] for ref in piece]
    other = jnp.broadcast_to(depth_ref[...].astype(F32), (rows, rows))
    other = jnp.where(iota((rows, rows), 0) == iota((rows, rows), 1), other, 0.0)
    other = jnp.broadcast_to(jnp.sum(other, axis=1, keepdims=True), (rows, LANES))
    depths[...] = jnp.concatenate([tail[0], other, jnp.zeros((8, LANES), F32)], 0)
    half = lax.rem(chip, 16 // chip_rows)
    for m in range(pieces):
        for i in range(rows):
            begin = i * total + chip * chip_rows - half * chip_rows
            two = piece[m][pl.ds(pl.multiple_of(begin, 16), 16), :].astype(F32)
            one = two[:chip_rows]
            for k in range(1, 16 // chip_rows):
                one = jnp.where(half == k, two[k * chip_rows : (k + 1) * chip_rows], one)
            at = (i * pieces + m) * chip_rows
            window[at : at + chip_rows, :] = one
    mine = rows * pieces
    for j in range(chip_rows):
        picked[j * mine : (j + 1) * mine, :] = window[
            pl.ds(j, mine, stride=chip_rows), :
        ].astype(BF16)
    count_lanes = chip_rows * mine
    lane = lax.rem(iota((mine, count_lanes), 1), mine)
    from_i = iota((mine, count_lanes), 0) == lax.rem(lane, pieces) * rows + lane // pieces
    lane = iota((16, count_lanes), 1) // mine
    from_j = iota((16, count_lanes), 0) == lax.bitwise_xor(lane, lax.rem(me, CORES) * rows)
    depth_i = jnp.concatenate(tail, 0).astype(BF16)
    depth_i = dot(depth_i, from_i.astype(F32).astype(BF16), 0, 0)[:8, :]
    depth_j = dot(depths[...].astype(BF16), from_j.astype(F32).astype(BF16), 0, 0)[:8, :]
    inverse_right = (1.0 / (epsilon + jnp.minimum(depth_i, depth_j)))[:1, :]
    for c in range(C):
        if c % some == 0:
            g = dot(w_ref[c * C : (c + some) * C, :], picked[...], 1, 1)
            g = (g * inverse_right).astype(BF16)
        for k in range(count_lanes // LANES):
            g_right[k * C : (k + 1) * C, c * LANES : (c + 1) * LANES] = g[
                c % some * C : (c % some + 1) * C, k * LANES : (k + 1) * LANES
            ]
        feature = left_wide[pl.ds(c, pieces, stride=C), :]
        turns = [feature] + [pltpu.roll(feature, k * alignment, 1) for k in range(1, rows)]
        block_of = iota((pieces, LANES), 1) // alignment
        for j in range(group):
            both = jnp.concatenate(
                [jnp.where(block_of == j, turns[(j - i) % rows], 0.0) for i in range(rows)], 0
            )
            at = c * LANES + j * mine
            weights[at : at + mine, :] = both.astype(BF16)
    right_grad = dot(g_right[...], weights[...], 1, 0)
    in_tile = iota((8, LANES), 1) // C
    row_of = (iota((8, LANES), 0) * group + in_tile).astype(F32)
    for k in range(count_lanes // LANES):
        part = right_grad[k * C : (k + 1) * C, :]
        stage[...] = jnp.concatenate([part] * group, 0).T
        for j in range(group):
            flat = jnp.zeros((8, LANES), F32)
            for q in range(group):
                flat = jnp.where(
                    in_tile == q, stage[pl.ds(j * alignment + q, tiles, stride=group), :], flat
                )
            residue = lax.bitwise_xor(k * group + j, lax.rem(me, CORES) * rows)
            depth = depths[pl.ds(residue, 1), :]
            at = (k * group + j) * tiles
            out_ref[at : at + tiles, :] = jnp.where(row_of < depth, flat, 0.0)


def main_kernel(sizes, *refs):
    rows, total, pieces, used, arrays, route = sizes
    piece = views(refs[:arrays], used)
    own_ref, other_ref, right_ref, cots, left_halves = refs[arrays : arrays + 5]
    partial_ref, spread, outer, inverse_own = refs[arrays + 5 : arrays + 9]
    turned, inverse = refs[arrays + 9 :]
    pairs = rows * total
    tiles = C * C // LANES
    per_tile = LANES // total
    me = lax.axis_index("pi")
    at_pairs = pairs + C + tiles * rows

    half = total // CORES
    row = iota((total, LANES), 0)
    core = lax.rem(me, CORES)
    step = jnp.zeros((total, LANES), jnp.int32)
    for m, offset in enumerate(offsets(route)):
        for k in range(CORES):
            at = row // rows == k * pieces + m
            step = jnp.where(at, jnp.where(core == k, offset[0], offset[1]) + k, step)
    source = lax.bitwise_xor(step, me) * rows + lax.rem(row, rows)
    place = (source == lax.rem(iota((total, LANES), 1), total)).astype(F32).astype(BF16)
    both = [
        jnp.concatenate([ref[t * half : (t + 1) * half, :] for ref in (own_ref, other_ref)], 0)
        for t in range(tiles + 1)
    ]
    for tile in range(tiles):
        turned[tile * LANES : (tile + 1) * LANES, :] = dot(both[tile], place, 0, 0)
    depth_lane = dot(both[tiles], place, 0, 0)

    for m in range(pieces):
        block = piece[m][at_pairs : at_pairs + 16, :].astype(F32)
        for tile in range(pairs // LANES):
            least = jnp.minimum(block[8 + tile : 9 + tile, :], depth_lane[:1, :])
            inverse[m : m + 1, tile * LANES : (tile + 1) * LANES] = 1.0 / (epsilon + least)

    alignment = spread.shape[0] // per_tile
    alive = iota((alignment, LANES), 0).astype(F32) < depth_lane[:alignment, :]
    part_of = iota((alignment, LANES), 1) // total
    keep = [jnp.where(alive & (part_of == k), 1.0, 0.0).astype(F32) for k in range(per_tile)]
    for d in range(C):
        block = turned[pl.ds(d, alignment, stride=C), :]
        for k in range(per_tile):
            spread[k * alignment : (k + 1) * alignment, d * LANES : (d + 1) * LANES] = (
                block * keep[k]
            ).astype(BF16)

    chunk = 8
    for d in range(C):
        if d % 2 == 0:
            two = spread[:, d * LANES : (d + 2) * LANES]
            parts = [
                dot(left_halves[h * pieces * C : (h + 1) * pieces * C, :], two, 1, 0)
                for h in range(pairs // LANES)
            ]
        for h in range(pairs // LANES):
            o = parts[h][:, d % 2 * LANES : (d % 2 + 1) * LANES]
            count = inverse[:, h * LANES : (h + 1) * LANES]
            for m in range(pieces):
                at = m * pairs + h * LANES
                outer[d * C : (d + 1) * C, at : at + LANES] = (
                    o[m * C : (m + 1) * C, :] * count[m : m + 1, :]
                ).astype(BF16)
        if d % chunk == chunk - 1:
            first = d + 1 - chunk
            some = slice(first * C, (d + 1) * C)
            grad = dot(outer[some, :], cots[...], 1, 0)
            for k in range(chunk):
                partial_ref[pl.ds(first + k, C, stride=C), :] = grad[k * C : (k + 1) * C, :]
    wide = C * C
    last = wide + right_ref.shape[0]
    partial_ref[wide:last, :] = right_ref[...]
    partial_ref[last : last + 8, :] = dot(
        jnp.ones((8, pieces * pairs), BF16), cots[...], 1, 0
    )
    inverse_own[...] = inverse[...]


def own_kernel(
    rows, spread, outer, inverse_own, payload_ref, w_swap_ref, bias_ref,
    update_ref, left_ref, g_left, stage,
):
    some = 8
    pairs = update_ref.shape[0]
    tiles = left_ref.shape[1] // LANES
    alignment = tiles * (LANES // C)
    halves = pairs // LANES
    group = LANES // C
    update = dot(outer[:, :pairs], w_swap_ref[...], 0, 0)
    update_ref[...] = (update + bias_ref[...]).astype(BF16)
    for d in range(C):
        if d % some == 0:
            g = dot(w_swap_ref[d * C : (d + some) * C, :], payload_ref[:pairs, :], 1, 1)
            g = (g * inverse_own[:1, :]).astype(BF16)
        for h in range(halves):
            g_left[h * C : (h + 1) * C, d * LANES : (d + 1) * LANES] = g[
                d % some * C : (d % some + 1) * C, h * LANES : (h + 1) * LANES
            ]
    left_grad = dot(spread[...], g_left[...], 1, 1)
    for h in range(halves):
        part = left_grad[:, h * C : (h + 1) * C]
        stage[h * spread.shape[0] : (h + 1) * spread.shape[0], :] = jnp.concatenate(
            [part] * group, 1
        )
    in_tile = iota((8, LANES), 1) // C
    row_of = (iota((8, LANES), 0) * group + in_tile).astype(F32)
    at_depth = pairs + C + tiles * rows
    depth = payload_ref[at_depth : at_depth + 16, :].astype(F32)
    for i in range(rows):
        flat = jnp.zeros((8, LANES), F32)
        for q in range(group):
            flat = jnp.where(
                in_tile == q, stage[pl.ds(i * alignment + q, tiles, stride=group), :], flat
            )
        flat = jnp.where(row_of < depth[i : i + 1, :], flat, 0.0)
        for tile in range(tiles):
            left_ref[i : i + 1, tile * LANES : (tile + 1) * LANES] = flat[tile : tile + 1, :]


def swap(x, masks, size):
    return lax.ppermute(x, "pi", [(i, i ^ masks[i % CORES]) for i in range(size)])


def route_of(size):
    near, middle, far = CORES, size // 4, size // 2
    if near * 2 == middle:
        return (
            ((0,), (far,) * CORES),
            ((0,), (far + middle + near,) * CORES),
            ((1,), (middle,) * CORES),
            ((0,), (near,) * CORES),
            ((4,), (middle,) * CORES),
            ((0,), (middle,) * CORES),
            ((1,), (near,) * CORES),
        )
    return tuple(((0,), (offset,) * CORES) for offset in range(CORES, size, CORES))


def offsets(route):
    found = [(0,) * CORES]
    for sources, hops in route:
        found += [tuple(a ^ b for a, b in zip(found[k], hops)) for k in sources]
    return found


def gathered(left, right, depth, w_out, bias, pair_cot):
    rows, width = left.shape
    alignment = width // C
    total, channels = pair_cot.shape[1:]
    size = lax.axis_size("pi")
    pieces = size // CORES
    pairs = rows * total
    chip_rows = CORES * rows
    tiles = width // LANES
    used = pairs + C + tiles * rows + 16
    hbm = pl.BlockSpec(memory_space=pltpu.HBM)
    vmem = pl.BlockSpec(memory_space=pltpu.VMEM)
    depth_other = swap(depth, (1, 1), size)
    given = (
        left, right, pair_cot.reshape(pairs, channels), depth, bias.reshape(1, channels), w_out,
    )
    payload, bias_row, w_here = pl.pallas_call(
        pack_kernel,
        out_shape=(
            pltpu.VMEM((used, LANES), BF16),
            pltpu.VMEM((1, channels), F32),
            pltpu.VMEM(w_out.shape, BF16),
        ),
        in_specs=[hbm] * 6,
        out_specs=(vmem, vmem, vmem),
        scratch_shapes=[
            pltpu.VMEM(left.shape, BF16),
            pltpu.VMEM(right.shape, BF16),
            pltpu.SMEM(depth.shape, jnp.int32),
            pltpu.SemaphoreType.DMA((6,)),
        ],
        compiler_params=pltpu.CompilerParams(vmem_limit_bytes=SMALL),
        cost_estimate=pl.CostEstimate(flops=10**9, bytes_accessed=2**20, transcendentals=0),
    )(*[pltpu.with_memory_space_constraint(x, pltpu.HBM) for x in given])
    arrived = [payload]
    place = {0: payload}
    route = route_of(size)
    for sources, hops in route:
        message = [place[k] for k in sources]
        message = swap(jnp.concatenate(message, 0) if len(message) > 1 else message[0], hops, size)
        if len(sources) == 1:
            place[sum(x.shape[0] for x in arrived) // used] = message
        arrived.append(message)
    mine = pl.pallas_call(
        functools.partial(collect_kernel, used, pairs + C),
        out_shape=pltpu.VMEM((total // CORES * (tiles + 1), LANES), BF16),
        compiler_params=pltpu.CompilerParams(vmem_limit_bytes=SMALL),
    )(*arrived)
    theirs = swap(mine, (1, 1), size)
    count_lanes = chip_rows * rows * pieces
    per_tile = LANES // total
    right_partial, cots, left_halves, w_swap = pl.pallas_call(
        functools.partial(right_kernel, (rows, total, pieces, alignment, used, len(arrived))),
        out_shape=(
            pltpu.VMEM((chip_rows * tiles, LANES), F32),
            pltpu.VMEM((pieces * pairs, channels), BF16),
            pltpu.VMEM((rows // per_tile * pieces * C, per_tile * alignment), BF16),
            pltpu.VMEM(w_out.shape, BF16),
        ),
        scratch_shapes=[
            pltpu.VMEM((pieces * C, LANES), F32),
            pltpu.VMEM((count_lanes, channels), F32),
            pltpu.VMEM((count_lanes, channels), BF16),
            pltpu.VMEM((C * LANES, LANES), BF16),
            pltpu.VMEM((count_lanes // LANES * C, C * LANES), BF16),
            pltpu.VMEM((LANES, LANES), F32),
            pltpu.VMEM((16, LANES), F32),
            pltpu.VMEM(w_out.shape, F32),
        ],
        compiler_params=pltpu.CompilerParams(vmem_limit_bytes=LARGE),
        cost_estimate=pl.CostEstimate(flops=10**9, bytes_accessed=2**20, transcendentals=0),
    )(*arrived, w_here, depth_other.reshape(1, rows))
    partial, spread, outer, inverse_own = pl.pallas_call(
        functools.partial(main_kernel, (rows, total, pieces, used, len(arrived), route)),
        out_shape=(
            pltpu.VMEM((C * C + chip_rows * tiles + 8, LANES), F32),
            pltpu.VMEM((per_tile * alignment, C * LANES), BF16),
            pltpu.VMEM((C * C, pieces * pairs), BF16),
            pltpu.VMEM((pieces, pairs), F32),
        ),
        scratch_shapes=[
            pltpu.VMEM((width, LANES), F32),
            pltpu.VMEM((pieces, pairs), F32),
        ],
        compiler_params=pltpu.CompilerParams(vmem_limit_bytes=LARGE),
    )(*arrived, mine, theirs, right_partial, cots, left_halves)
    other = swap(partial, (1, 1), size)
    update, grad_left = pl.pallas_call(
        functools.partial(own_kernel, rows),
        out_shape=(pltpu.VMEM((pairs, channels), BF16), pltpu.VMEM((rows, width), F32)),
        scratch_shapes=[
            pltpu.VMEM((pairs // LANES * C, C * LANES), BF16),
            pltpu.VMEM((LANES, LANES), F32),
        ],
        compiler_params=pltpu.CompilerParams(vmem_limit_bytes=LARGE),
        cost_estimate=pl.CostEstimate(
            flops=8 * pairs * C * C * channels, bytes_accessed=4 * 2**20, transcendentals=0
        ),
    )(spread, outer, inverse_own, payload, w_swap, bias_row)
    update, grad_left, grad_w, grad_right, grad_bias = pl.pallas_call(
        functools.partial(sum_kernel, rows),
        out_shape=(
            jax.ShapeDtypeStruct((pairs, channels), BF16),
            jax.ShapeDtypeStruct((rows, width), F32),
            jax.ShapeDtypeStruct((C * C, channels), F32),
            jax.ShapeDtypeStruct((rows, width), F32),
            jax.ShapeDtypeStruct((1, channels), F32),
        ),
        out_specs=(hbm,) * 5,
        scratch_shapes=[
            pltpu.VMEM((C * C, channels), F32),
            pltpu.VMEM((rows, width), F32),
            pltpu.VMEM((1, channels), F32),
            pltpu.SemaphoreType.DMA((8,)),
        ],
        compiler_params=pltpu.CompilerParams(vmem_limit_bytes=SMALL),
    )(partial, other, update, grad_left)
    return (
        update.reshape(rows, total, channels),
        grad_left,
        grad_right,
        grad_w,
        grad_bias.reshape(channels),
    )


def gathers(left, pair_cot, w_out):
    rows, width = left.shape
    total, channels = pair_cot.shape[1:]
    size = lax.axis_size("pi")
    gather_bytes = size * pair_cot.size * 2
    reduce_bytes = 2 * w_out.size * 4
    return (
        gather_bytes <= reduce_bytes
        and size >= 2 * CORES
        and size & (size - 1) == 0
        and rows & (rows - 1) == 0
        and channels == LANES
        and rows * (width // C) == LANES
        and LANES % total == 0
        and width == C * C == 8 * LANES
        and rows * CORES == 8
        and (rows * size // CORES) * (LANES // C) == LANES
    )


def local(left, right, depth, w_out, bias, pair_cot):
    if gathers(left, pair_cot, w_out):
        return gathered(left, right, depth, w_out, bias, pair_cot)
    return reduced(left, right, depth, w_out, bias, pair_cot)


def reduced(left, right, depth, w_out, bias, pair_cot):
    rows = left.shape[0]
    width = left.shape[1]
    alignment = width // C
    total = pair_cot.shape[1]
    channels = w_out.shape[1]
    row_ids = jnp.arange(alignment, dtype=jnp.int32)
    own_mask = (row_ids[None, :] < depth[:, None]).astype(jnp.bfloat16)
    own_left = left.reshape(rows, alignment, C) * own_mask[:, :, None]
    w_back = w_out.T
    pair_cols = lax.all_to_all(pair_cot, "pi", split_axis=1, concat_axis=0, tiled=True)
    init = (
        jnp.zeros((rows, total, channels), jnp.bfloat16),
        jnp.zeros((rows, width), jnp.float32),
        jnp.zeros((C * C, channels), jnp.float32),
        jnp.zeros((channels,), jnp.float32),
    )
    carry = init
    start = jnp.int32(0)
    right_piece = lax.all_gather(right, "pi", axis=0, tiled=True)
    depth_piece = lax.all_gather(depth, "pi", axis=0, tiled=True)
    length = right_piece.shape[0]
    block = math.gcd(length, 256)
    for offset in range(0, length, block):
        begin = start + offset
        depth_block = depth_piece[offset : offset + block]
        mask_block = (row_ids[None, :] < depth_block[:, None]).astype(jnp.bfloat16)
        right_block = (
            right_piece[offset : offset + block].reshape(block, alignment, C)
            * mask_block[:, :, None]
        )
        count = epsilon + jnp.minimum(depth[:, None], depth_block[None, :]).astype(jnp.float32)
        outer = jnp.einsum(
            "isc,jsd->ijcd", own_left, right_block, preferred_element_type=jnp.float32
        )
        outer = (outer / count[:, :, None, None]).reshape(rows, block, C * C).astype(jnp.bfloat16)
        update = (jnp.dot(outer, w_out, preferred_element_type=jnp.float32) + bias).astype(
            jnp.bfloat16
        )
        cot_block = lax.dynamic_slice_in_dim(pair_cot, begin, block, 1)
        pair_out = lax.dynamic_update_slice(carry[0], update, (0, begin, 0))
        weight_acc = carry[2] + jnp.dot(
            outer.reshape(-1, C * C).T,
            cot_block.reshape(-1, channels),
            preferred_element_type=jnp.float32,
        )
        bias_acc = carry[3] + jnp.sum(cot_block, axis=(0, 1), dtype=jnp.float32)
        grad_pair = (
            jnp.dot(cot_block, w_back, preferred_element_type=jnp.float32) / count[:, :, None]
        )
        grad_pair = grad_pair.astype(jnp.bfloat16).reshape(rows, block, C, C)
        left_acc = carry[1] + jnp.einsum(
            "ijcd,jsd->isc", grad_pair, right_block, preferred_element_type=jnp.float32
        ).reshape(rows, width)
        carry = (pair_out, left_acc, weight_acc, bias_acc)
    pair_update = carry[0]
    left_acc = carry[1]
    accum = jnp.zeros((rows, width), jnp.float32)
    start = jnp.int32(0)
    left_piece = lax.all_gather(left, "pi", axis=0, tiled=True)
    depth_piece = lax.all_gather(depth, "pi", axis=0, tiled=True)
    length = left_piece.shape[0]
    block = math.gcd(length, 256)
    for offset in range(0, length, block):
        begin = start + offset
        depth_block = depth_piece[offset : offset + block]
        mask_block = (row_ids[None, :] < depth_block[:, None]).astype(jnp.bfloat16)
        left_block = (
            left_piece[offset : offset + block].reshape(block, alignment, C)
            * mask_block[:, :, None]
        )
        count = epsilon + jnp.minimum(depth_block[:, None], depth[None, :]).astype(jnp.float32)
        cot_block = lax.dynamic_slice_in_dim(pair_cols, begin, block, 0)
        grad_pair = (
            jnp.dot(cot_block, w_back, preferred_element_type=jnp.float32) / count[:, :, None]
        )
        grad_pair = grad_pair.astype(jnp.bfloat16).reshape(block, rows, C, C)
        accum = accum + jnp.einsum(
            "ijcd,isc->jsd", grad_pair, left_block, preferred_element_type=jnp.float32
        ).reshape(rows, width)
    grad_w, grad_bias = lax.psum((carry[2], carry[3]), "pi")
    grad_left = (left_acc.reshape(rows, alignment, C) * own_mask[:, :, None]).reshape(rows, width)
    grad_right = (accum.reshape(rows, alignment, C) * own_mask[:, :, None]).reshape(rows, width)
    return (pair_update, grad_left, grad_right, grad_w, grad_bias)


def solution(mesh):
    placed = (
        P(("grp", "pi"), None),
        P(("grp", "pi"), None),
        P(("grp", "pi")),
        P(),
        P(),
        P(("grp", "pi"), None, None),
    )
    return jax.shard_map(
        local,
        mesh=mesh,
        in_specs=placed,
        out_specs=(
            P(("grp", "pi"), None, None),
            P(("grp", "pi"), None),
            P(("grp", "pi"), None),
            P("grp", None),
            P("grp"),
        ),
        check_vma=False,
    )
```
